32 devices in a mesh: tok: 8 (over y, x, core), mlp: 4 (over z).
Axes of the slice: x: 2, y: 2, z: 4, core: 2. Of those that a mesh axis runs over, the one named last changes fastest.
Arguments:
- layer_input: bfloat16 [4096, 4096], P('tok'), may hold values from -80 to 80
- input_norm_gain: float32 [4096], replicated, may hold values from 0.6 to 10
- query_weight: bfloat16 [4096, 4096], P(None, 'mlp'), may hold values from -0.09375 to 0.09375
- key_weight: bfloat16 [4096, 1024], P(None, 'mlp'), may hold values from -0.09375 to 0.09375
- value_weight: bfloat16 [4096, 1024], P(None, 'mlp'), may hold values from -0.09375 to 0.09375
- query_down_maps: bfloat16 [256, 16, 4096], P('tok', None, 'mlp'), may hold values from -0.09375 to 0.09375
- value_down_maps: bfloat16 [256, 16, 4096], P('tok', None, 'mlp'), may hold values from -0.09375 to 0.09375
- query_up_maps: bfloat16 [256, 16, 4096], P('tok', None, 'mlp'), may hold values from -1.5 to 1.5
- value_up_maps: bfloat16 [256, 16, 1024], P('tok', None, 'mlp'), may hold values from -1.5 to 1.5
- tenant_prompt_length: int32 [16], replicated, may hold values from 1 to 2048, 4096 in all
- tenant_adapter_id: int32 [16], replicated, may hold values from 0 to 255
- adapter_storage_slot: int32 [256], replicated, may hold values from 0 to 255, each once
Outputs:
- attended: bfloat16 [4096, 4096], P('tok', 'mlp')
The draws below stay inside these ranges and needn't reach their ends.
Inputs may be any that keep to these rules, and one draw needn't show every extreme that they name: `tenant_prompt_length`: the lengths sum to 4096; each is at most 2048 and one of them is exactly that. `tenant_adapter_id`: tenants may share an adapter. `adapter_storage_slot`: each storage slot holds exactly one adapter.
All inputs are finite; a program needn't handle non-finite values.
Results may differ from the reference program's by a relative error of at most 0.0045.
The reference program's roundings to bfloat16 on the way count: a program that leaves them out, or rounds other values in their place, can miss the bound.
Values may be sent and summed in bfloat16 or wider, within the bound.
No kernel may reach another device: no remote copies, remote signals or barrier semaphores. Data moves between devices by JAX's collectives and lax.ppermute only.
A program may use at most 192 MiB of HBM per device.

```python
import math
import jax
import jax.numpy as jnp
import numpy as np
from jax import lax

MODEL_WIDTH = 4096
QUERY_HEADS = 32
KEY_VALUE_HEADS = 8
HEAD_WIDTH = 128
ADAPTER_RANK = 16
ADAPTER_COUNT = 256
TENANTS = 16
LONGEST_PROMPT = 4
TOKENS_PER_PART = 512
TOKENS = 4096
N_TOK = 8


def draw_layer_input(key, part):
    streams = jax.random.split(key, 1)
    values = jnp.clip(jax.random.normal(streams[0], (TOKENS, MODEL_WIDTH), jnp.float32), -6.0, 6.0)
    return values.astype(jnp.bfloat16)


def draw_input_norm_gain(key, part):
    values = jax.random.uniform(key, (MODEL_WIDTH,), jnp.float32, 0.6, 1.6)
    return values


def plant(array, rng, least, largest):
    shape = array.shape
    place = [jax.random.randint(jax.random.fold_in(rng, axis), (), 0, shape[axis]) for axis in range(len(shape))]
    array = array.at[tuple(place)].set(least)
    longest = shape.index(max(shape))
    place[longest] = (place[longest] + 1) % shape[longest]
    return array.at[tuple(place)].set(largest)


def block_scale(own_key, shape, pieces, least, top_value):
    def one(position, blocks):
        draws = jax.random.uniform(jax.random.fold_in(jax.random.fold_in(own_key, 6), position), (blocks,), jnp.float32, least / len(pieces), top_value / len(pieces))
        return jnp.repeat(jnp.exp(draws), shape[position] // blocks).reshape((-1,) + (1,) * (len(shape) - position - 1))

    loudness = one(*pieces[0])
    for cut in pieces[1:]:
        loudness = loudness * one(*cut)
    return loudness


def profile(number_of, total, limit, lean):
    weights = [(1 << 20) // math.isqrt(grade ** lean) + 1 for grade in range(2, number_of + 1)]
    surplus, holding = total - limit - (number_of - 1), [1] * (number_of - 1)
    while surplus > 0:
        candidates = [i for i in range(number_of - 1) if holding[i] < limit]
        whole, left = sum([weights[i] for i in candidates]), surplus
        for i in candidates:
            extra = min(limit - holding[i], max(1, left * weights[i] // whole), surplus)
            holding[i] = holding[i] + extra
            surplus = surplus - extra
    return np.array([limit] + holding)


def uneven_parts(own_key, count, total, most, skew):
    if count == 2:
        one = jax.random.randint(own_key, (), max(1, total - most), min(most, total - 1) + 1)
        return jnp.stack([one, total - one])
    sizes = jnp.asarray(profile(count, total, most, skew), jnp.int32)
    couples = (count - 1) // 2
    source_of, receiver = sizes[1:1 + 2 * couples:2], sizes[2:2 + 2 * couples:2]
    margin = jnp.minimum(source_of - 1, most - receiver)
    passed = jax.random.randint(jax.random.fold_in(own_key, 1), (couples,), 0, 1 << 20) % (margin + 1)
    sizes = sizes.at[1:1 + 2 * couples:2].set(source_of - passed).at[2:2 + 2 * couples:2].set(receiver + passed)
    return sizes[jax.random.permutation(jax.random.fold_in(own_key, 2), count)]


def gaussian(rng, shape, deviation, most, cuts=(), held_as=jnp.bfloat16):
    gain = block_scale(rng, shape, cuts, -0.22, 0.18) if cuts else 1.0
    array = jax.random.normal(rng, shape, jnp.float32) * deviation * gain
    return jnp.minimum(jnp.maximum(array, -most), most).astype(held_as)


def setup_inputs(seed: int = 0) -> dict:
    keys = jax.random.split(jax.random.key(seed), 13)
    layer_input = draw_layer_input(jax.random.fold_in(keys[12], 71), 0)
    input_norm_gain = draw_input_norm_gain(jax.random.fold_in(keys[12], 71), 0)
    query_weight = gaussian(keys[2], (MODEL_WIDTH, QUERY_HEADS * HEAD_WIDTH), MODEL_WIDTH ** -0.5, 0.09375, ((1, 4),))
    key_weight = gaussian(keys[3], (MODEL_WIDTH, KEY_VALUE_HEADS * HEAD_WIDTH), MODEL_WIDTH ** -0.5, 0.09375, ((1, 4),))
    value_weight = gaussian(keys[4], (MODEL_WIDTH, KEY_VALUE_HEADS * HEAD_WIDTH), MODEL_WIDTH ** -0.5, 0.09375, ((1, 4),))
    query_down_maps = gaussian(keys[5], (ADAPTER_COUNT, ADAPTER_RANK, MODEL_WIDTH), MODEL_WIDTH ** -0.5, 0.09375, ((0, 8), (2, 4)))
    value_down_maps = gaussian(keys[6], (ADAPTER_COUNT, ADAPTER_RANK, MODEL_WIDTH), MODEL_WIDTH ** -0.5, 0.09375, ((0, 8), (2, 4)))
    query_up_maps = gaussian(keys[7], (ADAPTER_COUNT, ADAPTER_RANK, QUERY_HEADS * HEAD_WIDTH), ADAPTER_RANK ** -0.5, 1.5, ((0, 8), (2, 4)))
    value_up_maps = gaussian(keys[8], (ADAPTER_COUNT, ADAPTER_RANK, KEY_VALUE_HEADS * HEAD_WIDTH), ADAPTER_RANK ** -0.5, 1.5, ((0, 8), (2, 4)))
    tenant_prompt_length = uneven_parts(keys[9], TENANTS, TOKENS, LONGEST_PROMPT * TOKENS_PER_PART, 2).astype(jnp.int32)
    tenant_adapter_id = plant(jax.random.randint(keys[10], (TENANTS,), 0, ADAPTER_COUNT), jax.random.fold_in(keys[10], 1), 0, ADAPTER_COUNT - 1).astype(jnp.int32)
    adapter_storage_slot = jax.random.permutation(keys[11], ADAPTER_COUNT).astype(jnp.int32)
    return {"layer_input": layer_input, "input_norm_gain": input_norm_gain, "query_weight": query_weight, "key_weight": key_weight, "value_weight": value_weight, "query_down_maps": query_down_maps, "value_down_maps": value_down_maps, "query_up_maps": query_up_maps, "value_up_maps": value_up_maps, "tenant_prompt_length": tenant_prompt_length, "tenant_adapter_id": tenant_adapter_id, "adapter_storage_slot": adapter_storage_slot}


NORM_EPS = 1e-05
ROPE_BASE = 500000.0
ADAPTER_SCALE = 0.5

def rotary(values, positions):
    half_width = values.shape[-1] // 2
    exponent = jnp.arange(half_width).astype(jnp.float32) * (2.0 / values.shape[-1])
    inverse = jnp.exp(-exponent * jnp.log(jnp.float32(ROPE_BASE)))
    angles = positions.astype(jnp.float32)[:, None] * inverse[None, :]
    cosine = jnp.cos(angles)[:, None, :]
    sine = jnp.sin(angles)[:, None, :]
    first_position = values[..., :half_width]
    second = values[..., half_width:]
    return jnp.concatenate([first_position * cosine - second * sine, second * cosine + first_position * sine], axis=-1)

def tenant_of(tenant_prompt_length, indices):
    prompt_ends = jnp.cumsum(tenant_prompt_length).astype(jnp.int32)
    prompt_starts = prompt_ends - tenant_prompt_length
    tenant_ids = lax.optimization_barrier(jnp.sum((indices[:, None] >= prompt_ends[None, :]).astype(jnp.int32), axis=1))
    member = tenant_ids[:, None] == jnp.arange(tenant_prompt_length.shape[0], dtype=jnp.int32)[None, :]
    row_start = lax.optimization_barrier(jnp.sum(jnp.where(member, prompt_starts[None, :], 0), axis=1)).astype(jnp.int32)
    return (member, row_start)

def projections(normed_input, chosen, positions, query_weight, key_weight, value_weight, shrink_q, shrink_v, query_up_table, value_up_table):
    row_count = normed_input.shape[0]
    shrink_q = jnp.where(chosen, shrink_q, 0.0).astype(jnp.bfloat16)
    shrink_v = jnp.where(chosen, shrink_v, 0.0).astype(jnp.bfloat16)
    query_delta = jnp.dot(shrink_q, query_up_table.reshape(-1, query_up_table.shape[2]), preferred_element_type=jnp.float32)
    value_delta = jnp.dot(shrink_v, value_up_table.reshape(-1, value_up_table.shape[2]), preferred_element_type=jnp.float32)
    query_rows = jnp.dot(normed_input, query_weight, preferred_element_type=jnp.float32) + ADAPTER_SCALE * query_delta
    query_rows = rotary(query_rows.reshape(row_count, -1, HEAD_WIDTH), positions).astype(jnp.bfloat16)
    key = jnp.dot(normed_input, key_weight, preferred_element_type=jnp.float32)
    key = rotary(key.reshape(row_count, -1, HEAD_WIDTH), positions).astype(jnp.bfloat16)
    value_rows = jnp.dot(normed_input, value_weight, preferred_element_type=jnp.float32) + ADAPTER_SCALE * value_delta
    value_rows = value_rows.astype(jnp.bfloat16).reshape(row_count, -1, HEAD_WIDTH)
    return (query_rows, key, value_rows)

def contract(left, table):
    flat = table.reshape(-1, table.shape[2])
    return lax.dot_general(left, flat, (((1,), (1,)), ((), ())), preferred_element_type=jnp.float32)

def attend(query_rows, key, value_rows, row_start):
    span = (LONGEST_PROMPT + 1) * TOKENS_PER_PART
    head_groups = QUERY_HEADS // KEY_VALUE_HEADS
    padding_rows = jnp.zeros((LONGEST_PROMPT * TOKENS_PER_PART, KEY_VALUE_HEADS, HEAD_WIDTH), jnp.bfloat16)
    pad_key = jnp.concatenate([padding_rows, key], axis=0)
    pad_value = jnp.concatenate([padding_rows, value_rows], axis=0)

    def one_block(index):
        first_position = (index * TOKENS_PER_PART).astype(jnp.int32)
        query_block = lax.dynamic_slice_in_dim(query_rows, first_position, TOKENS_PER_PART, 0).astype(jnp.float32).reshape(TOKENS_PER_PART, KEY_VALUE_HEADS, head_groups, HEAD_WIDTH)
        k_block = lax.dynamic_slice_in_dim(pad_key, first_position, span, 0).astype(jnp.float32)
        v_block = lax.dynamic_slice_in_dim(pad_value, first_position, span, 0).astype(jnp.float32)
        starts = lax.dynamic_slice_in_dim(row_start, first_position, TOKENS_PER_PART, 0)
        q_index = first_position + jnp.arange(TOKENS_PER_PART, dtype=jnp.int32)
        k_index = first_position - LONGEST_PROMPT * TOKENS_PER_PART + jnp.arange(span, dtype=jnp.int32)
        allowed = (k_index[None, :] >= starts[:, None]) & (k_index[None, :] <= q_index[:, None])
        scores = jnp.einsum('qhgd,khd->hgqk', query_block, k_block) * HEAD_WIDTH ** (-0.5)
        scores = jnp.where(allowed[None, None], scores, -jnp.inf)
        peak = lax.optimization_barrier(jnp.max(scores, axis=-1, keepdims=True))
        weights = jnp.exp(scores - peak)
        totals = lax.optimization_barrier(jnp.sum(weights, axis=-1))
        rounded = lax.optimization_barrier(weights.astype(jnp.bfloat16)).astype(jnp.float32)
        mixed = jnp.einsum('hgqk,khd->qhgd', rounded, v_block)
        result = mixed / jnp.transpose(totals, (2, 0, 1))[..., None]
        return result.astype(jnp.bfloat16).reshape(TOKENS_PER_PART, QUERY_HEADS * HEAD_WIDTH)
    blocks = lax.map(one_block, jnp.arange(N_TOK, dtype=jnp.int32))
    return blocks.reshape(TOKENS, QUERY_HEADS * HEAD_WIDTH)

def reference(layer_input, input_norm_gain, query_weight, key_weight, value_weight, query_down_maps, value_down_maps, query_up_maps, value_up_maps, tenant_prompt_length, tenant_adapter_id, adapter_storage_slot):
    widened = layer_input.astype(jnp.float32)
    scale_row = lax.rsqrt(lax.optimization_barrier(jnp.mean(widened * widened, axis=1, keepdims=True)) + NORM_EPS)
    normed_input = (widened * scale_row * input_norm_gain.astype(jnp.float32)[None, :]).astype(jnp.bfloat16)
    indices = jnp.arange(TOKENS, dtype=jnp.int32)
    member, row_start = tenant_of(tenant_prompt_length, indices)
    positions = indices - row_start
    chosen = jnp.repeat(member, ADAPTER_RANK, axis=1)
    storage_slots = adapter_storage_slot[tenant_adapter_id]
    query_down_table = query_down_maps[storage_slots]
    value_down_table = value_down_maps[storage_slots]
    query_up_table = query_up_maps[storage_slots]
    value_up_table = value_up_maps[storage_slots]
    shrink_q = contract(normed_input, query_down_table)
    shrink_v = contract(normed_input, value_down_table)
    query_rows, key, value_rows = projections(normed_input, chosen, positions, query_weight, key_weight, value_weight, shrink_q, shrink_v, query_up_table, value_up_table)
    return attend(query_rows, key, value_rows, row_start)
```

```python
import functools
import math

import jax
import jax.numpy as jnp
from jax import lax
from jax.experimental import pallas as pl
from jax.experimental.pallas import tpu as pltpu
from jax.sharding import PartitionSpec as P

HEAD_WIDTH = 128
ADAPTER_RANK = 16
LONGEST_PROMPT = 4
NORM_EPS = 1e-05
ROPE_BASE = 500000.0
ADAPTER_SCALE = 0.5
VMEM_LIMIT = 56 * 1024 * 1024
TILE = 256
CHUNK = 512


def positions_of(tenant_prompt_length, indices):
    prompt_ends = jnp.cumsum(tenant_prompt_length)
    passed = jnp.where(indices[:, None] >= prompt_ends[None, :], prompt_ends[None, :], 0)
    return indices - jnp.max(passed, axis=1)


def rotary_tables(positions):
    half_width = HEAD_WIDTH // 2
    exponent = jnp.arange(half_width).astype(jnp.float32) * (2.0 / HEAD_WIDTH)
    inverse = jnp.exp(-exponent * jnp.log(jnp.float32(ROPE_BASE)))
    angles = positions.astype(jnp.float32)[:, None] * inverse[None, :]
    cosine = jnp.cos(angles)
    sine = jnp.sin(angles)
    return jnp.concatenate([cosine, cosine], axis=1), jnp.concatenate([-sine, sine], axis=1)


def rope(x, cosine, sine):
    half = HEAD_WIDTH // 2
    swapped = jnp.concatenate([x[:, half:], x[:, :half]], axis=1)
    return x * cosine + swapped * sine


def pick_kernel(tenants, id_ref, slot_ref, device_ref, qd, vd, qu, vu, first, second, sems):
    device = device_ref[0]
    core = lax.rem(device, 2)
    rank = ADAPTER_RANK
    held = qd.shape[0]
    wide = qd.shape[2] // 2
    narrow = vu.shape[2] // 2
    local = [slot_ref[id_ref[t]] - device * held for t in range(tenants)]

    def copies(t):
        made = []
        slot = jnp.clip(local[t], 0, held - 1)
        top = t * 2 * rank
        for side in range(2):
            half = core if side == 0 else 1 - core
            cols = pl.ds(pl.multiple_of(half * wide, 128), wide)
            few = pl.ds(pl.multiple_of(half * narrow, 128), narrow)
            pairs = (
                (qd.at[slot, :, cols], first.at[side, pl.ds(top, rank), pl.ds(0, wide)]),
                (vd.at[slot, :, cols], first.at[side, pl.ds(top + rank, rank), pl.ds(0, wide)]),
                (vu.at[slot, :, few], first.at[side, pl.ds(top, rank), pl.ds(wide, narrow)]),
                (qu.at[slot, :, cols], second.at[side, pl.ds(t * rank, rank), :]),
            )
            for number, (source, target) in enumerate(pairs):
                made.append(
                    pltpu.make_async_copy(source, target, sems.at[t, side * 4 + number])
                )
        return made

    for t in range(tenants):
        here = (local[t] >= 0) & (local[t] < held)
        top = t * 2 * rank

        @pl.when(here)
        def _(t=t):
            for copy in copies(t):
                copy.start()

        for side in range(2):
            first[side, top + rank : top + 2 * rank, wide:] = jnp.zeros(
                (rank, narrow), jnp.bfloat16
            )

        @pl.when(jnp.logical_not(here))
        def _(t=t, top=top):
            for side in range(2):
                first[side, top : top + 2 * rank, :wide] = jnp.zeros(
                    (2 * rank, wide), jnp.bfloat16
                )
                first[side, top : top + rank, wide:] = jnp.zeros((rank, narrow), jnp.bfloat16)
                second[side, t * rank : (t + 1) * rank, :] = jnp.zeros(
                    (rank, wide), jnp.bfloat16
                )

    for t in range(tenants):

        @pl.when((local[t] >= 0) & (local[t] < held))
        def _(t=t):
            for copy in copies(t):
                copy.wait()


def pick(ids, slots, device, qd, vd, qu, vu):
    tenants = ids.shape[0]
    held, rank, wide = qd.shape
    narrow = vu.shape[2]
    shapes = (
        (2, tenants * 2 * rank, (wide + narrow) // 2),
        (2, tenants * rank, wide // 2),
    )
    return pl.pallas_call(
        functools.partial(pick_kernel, tenants),
        grid_spec=pltpu.PrefetchScalarGridSpec(
            num_scalar_prefetch=3,
            grid=(1,),
            in_specs=[pl.BlockSpec(memory_space=pl.ANY)] * 4,
            out_specs=[pl.BlockSpec(shape, lambda i, *_: (0, 0, 0)) for shape in shapes],
            scratch_shapes=[pltpu.SemaphoreType.DMA((tenants, 8))],
        ),
        out_shape=[jax.ShapeDtypeStruct(shape, jnp.bfloat16) for shape in shapes],
        compiler_params=pltpu.CompilerParams(vmem_limit_bytes=VMEM_LIMIT),
        name="pick_adapters",
    )(ids, slots, device, qd, vd, qu, vu)


def project_kernel(
    share_ref,
    gain_ref,
    cos_ref,
    sin_ref,
    x_hbm,
    wk_hbm,
    wv_hbm,
    wq_hbm,
    key_hbm,
    value_hbm,
    query_hbm,
    share_hbm,
    x,
    normed,
    wk,
    wv,
    wq,
    key,
    value,
    query,
    in_sems,
    out_sems,
):
    rows, model = x.shape
    parts = 4
    step = rows // parts
    tile = wq.shape[2]
    tiles = wq.shape[0]
    width = HEAD_WIDTH
    arriving = [
        pltpu.make_async_copy(
            x_hbm.at[pl.ds(i * step, step), :], x.at[pl.ds(i * step, step), :], in_sems.at[i]
        )
        for i in range(parts)
    ]
    arriving.append(pltpu.make_async_copy(wk_hbm, wk, in_sems.at[parts]))
    arriving.append(pltpu.make_async_copy(wv_hbm, wv, in_sems.at[parts + 1]))
    for i in range(tiles):
        arriving.append(
            pltpu.make_async_copy(
                wq_hbm.at[:, pl.ds(i * tile, tile)], wq.at[i], in_sems.at[parts + 2 + i]
            )
        )
    for copy in arriving:
        copy.start()
    for i in range(parts):
        arriving[i].wait()
        at = slice(i * step, (i + 1) * step)
        wide = x[at, :].astype(jnp.float32)
        scale = lax.rsqrt(jnp.mean(wide * wide, axis=1, keepdims=True) + NORM_EPS)
        normed[at, :] = (wide * scale * gain_ref[...]).astype(jnp.bfloat16)
    leaving = []

    def leave(source, target):
        copy = pltpu.make_async_copy(source, target, out_sems.at[len(leaving)])
        copy.start()
        leaving.append(copy)

    kept = share_hbm.shape[1]
    leave(normed.at[:, pl.ds(pl.multiple_of(share_ref[0] * kept, 128), kept)], share_hbm)
    arriving[parts].wait()
    raw = jnp.dot(normed[...], wk[...], preferred_element_type=jnp.float32)
    for head in range(key.shape[1] // width):
        cols = slice(head * width, (head + 1) * width)
        key[:, cols] = rope(raw[:, cols], cos_ref[...], sin_ref[...]).astype(jnp.bfloat16)
    leave(key, key_hbm)
    arriving[parts + 1].wait()
    value[...] = jnp.dot(normed[...], wv[...], preferred_element_type=jnp.float32)
    leave(value, value_hbm)
    for i in range(tiles):
        arriving[parts + 2 + i].wait()
        query[i] = jnp.dot(normed[...], wq[i], preferred_element_type=jnp.float32)
        leave(query.at[i], query_hbm.at[:, pl.ds(i * tile, tile)])
    for copy in leaving:
        copy.wait()


def project(share, x, gain, wk, wv, wq, cosine, sine, shares):
    rows, model = x.shape
    kv_cols = wk.shape[1]
    q_cols = wq.shape[1]
    kept = model // shares
    tiles = q_cols // TILE
    whole = lambda i, s: (0, 0)
    return pl.pallas_call(
        project_kernel,
        grid_spec=pltpu.PrefetchScalarGridSpec(
            num_scalar_prefetch=1,
            grid=(1,),
            in_specs=[
                pl.BlockSpec((1, model), whole),
                pl.BlockSpec(cosine.shape, whole),
                pl.BlockSpec(sine.shape, whole),
            ]
            + [pl.BlockSpec(memory_space=pl.ANY)] * 4,
            out_specs=[pl.BlockSpec(memory_space=pl.ANY)] * 4,
            scratch_shapes=[
                pltpu.VMEM((rows, model), jnp.bfloat16),
                pltpu.VMEM((rows, model), jnp.bfloat16),
                pltpu.VMEM((model, kv_cols), jnp.bfloat16),
                pltpu.VMEM((model, kv_cols), jnp.bfloat16),
                pltpu.VMEM((tiles, model, TILE), jnp.bfloat16),
                pltpu.VMEM((rows, kv_cols), jnp.bfloat16),
                pltpu.VMEM((rows, kv_cols), jnp.float32),
                pltpu.VMEM((tiles, rows, TILE), jnp.float32),
                pltpu.SemaphoreType.DMA((6 + tiles,)),
                pltpu.SemaphoreType.DMA((3 + tiles,)),
            ],
        ),
        out_shape=[
            jax.ShapeDtypeStruct((rows, kv_cols), jnp.bfloat16),
            jax.ShapeDtypeStruct((rows, kv_cols), jnp.float32),
            jax.ShapeDtypeStruct((rows, q_cols), jnp.float32),
            jax.ShapeDtypeStruct((rows, kept), jnp.bfloat16),
        ],
        compiler_params=pltpu.CompilerParams(vmem_limit_bytes=VMEM_LIMIT),
        cost_estimate=pl.CostEstimate(
            flops=2 * rows * model * (q_cols + 2 * kv_cols),
            bytes_accessed=2 * model * (rows + q_cols + 2 * kv_cols),
            transcendentals=0,
        ),
        name="norm_and_projections",
    )(share, gain, cosine, sine, x, wk, wv, wq)


def tenant_at(length_ref, tenants, index):
    tid = jnp.zeros(index.shape, jnp.int32)
    start = jnp.zeros(index.shape, jnp.int32)
    end = 0
    for t in range(tenants):
        end = end + length_ref[t]
        past = index >= end
        tid = jnp.where(past, t + 1, tid)
        start = jnp.where(past, end, start)
    return tid, start


def shrink_kernel(tenants, device_ref, length_ref, own_ref, other_ref, x_own, x_other, out_ref):
    contract = (((1,), (1,)), ((), ()))
    half = x_own.shape[1]
    tokens = x_own.shape[0]
    wide = lax.dot_general(
        own_ref[:, :half], x_own[...], contract, preferred_element_type=jnp.float32
    )
    wide += lax.dot_general(
        other_ref[:, :half], x_other[...], contract, preferred_element_type=jnp.float32
    )
    rows = 2 * ADAPTER_RANK
    index = device_ref[0] * tokens + lax.broadcasted_iota(jnp.int32, (1, tokens), 1)
    tid, _ = tenant_at(length_ref, tenants, index)
    total = jnp.zeros((rows, tokens), jnp.float32)
    for t in range(tenants):
        total = total + jnp.where(tid == t, wide[t * rows : (t + 1) * rows, :], 0.0)
    out_ref[...] = total


def shrink(device, lengths, own, other, share):
    tenants = lengths.shape[0]
    tokens, kept = share.shape
    half = kept // 2
    whole = lambda i, *_: (0, 0)
    return pl.pallas_call(
        functools.partial(shrink_kernel, tenants),
        grid_spec=pltpu.PrefetchScalarGridSpec(
            num_scalar_prefetch=2,
            grid=(1,),
            in_specs=[
                pl.BlockSpec(own.shape, whole),
                pl.BlockSpec(other.shape, whole),
                pl.BlockSpec((tokens, half), lambda i, d, n: (0, lax.rem(d[0], 2))),
                pl.BlockSpec((tokens, half), lambda i, d, n: (0, 1 - lax.rem(d[0], 2))),
            ],
            out_specs=pl.BlockSpec((2 * ADAPTER_RANK, tokens), whole),
        ),
        out_shape=jax.ShapeDtypeStruct((2 * ADAPTER_RANK, tokens), jnp.float32),
        compiler_params=pltpu.CompilerParams(vmem_limit_bytes=VMEM_LIMIT),
        name="shrink_share",
    )(device, lengths, own, other, share, share)


def spread_tenants(shrunk, device_ref, length_ref, tenants):
    tokens = shrunk.shape[1]
    index = device_ref[0] * tokens + lax.broadcasted_iota(jnp.int32, (1, tokens), 1)
    tid, _ = tenant_at(length_ref, tenants, index)
    return jnp.concatenate(
        [jnp.where(tid == t, shrunk, 0.0).astype(jnp.bfloat16) for t in range(tenants)], axis=0
    )


def value_kernel(
    tenants, device_ref, length_ref, one_ref, two_ref, own_ref, other_ref, raw_ref, out_ref
):
    rank = ADAPTER_RANK
    shrunk = one_ref[rank:, :] + two_ref[rank:, :]
    spread = spread_tenants(shrunk, device_ref, length_ref, tenants)
    even = lax.rem(device_ref[0], 2) == 0
    for group in range(2):
        cols = slice(group * HEAD_WIDTH, (group + 1) * HEAD_WIDTH)
        mine = even if group == 0 else jnp.logical_not(even)
        kept = []
        for t in range(tenants):
            at = slice(2 * t * rank, (2 * t + 1) * rank)
            kept.append(jnp.where(mine, own_ref[at, :], other_ref[at, :]))
        delta = lax.dot_general(
            spread,
            jnp.concatenate(kept, axis=0),
            (((0,), (0,)), ((), ())),
            preferred_element_type=jnp.float32,
        )
        out_ref[:, cols] = (raw_ref[:, cols] + ADAPTER_SCALE * delta).astype(jnp.bfloat16)


def finish_value(device, lengths, one, two, own, other, raw):
    tenants = lengths.shape[0]
    whole = lambda i, *_: (0, 0)
    side = own.shape[1] // HEAD_WIDTH - 1
    return pl.pallas_call(
        functools.partial(value_kernel, tenants),
        grid_spec=pltpu.PrefetchScalarGridSpec(
            num_scalar_prefetch=2,
            grid=(1,),
            in_specs=[
                pl.BlockSpec(one.shape, whole),
                pl.BlockSpec(two.shape, whole),
                pl.BlockSpec((own.shape[0], HEAD_WIDTH), lambda i, *_: (0, side)),
                pl.BlockSpec((own.shape[0], HEAD_WIDTH), lambda i, *_: (0, side)),
                pl.BlockSpec(raw.shape, whole),
            ],
            out_specs=pl.BlockSpec(raw.shape, whole),
        ),
        out_shape=jax.ShapeDtypeStruct(raw.shape, jnp.bfloat16),
        compiler_params=pltpu.CompilerParams(vmem_limit_bytes=VMEM_LIMIT),
        name="value_rows",
    )(device, lengths, one, two, own, other, raw)


def query_kernel(
    tenants,
    device_ref,
    length_ref,
    one_ref,
    two_ref,
    own_ref,
    other_ref,
    raw_ref,
    cos_ref,
    sin_ref,
    out_ref,
):
    rank = ADAPTER_RANK
    shrunk = one_ref[:rank, :] + two_ref[:rank, :]
    spread = spread_tenants(shrunk, device_ref, length_ref, tenants)
    even = lax.rem(device_ref[0], 2) == 0
    half = own_ref.shape[1]
    for group in range(2):
        mine = even if group == 0 else jnp.logical_not(even)
        delta = lax.dot_general(
            spread,
            jnp.where(mine, own_ref[...], other_ref[...]),
            (((0,), (0,)), ((), ())),
            preferred_element_type=jnp.float32,
        )
        for head in range(half // HEAD_WIDTH):
            local = slice(head * HEAD_WIDTH, (head + 1) * HEAD_WIDTH)
            at = group * half + head * HEAD_WIDTH
            cols = slice(at, at + HEAD_WIDTH)
            row = raw_ref[:, cols] + ADAPTER_SCALE * delta[:, local]
            out_ref[:, cols] = rope(row, cos_ref[...], sin_ref[...]).astype(jnp.bfloat16)


def finish_query(device, lengths, one, two, own, other, raw, cosine, sine):
    tenants = lengths.shape[0]
    whole = lambda i, *_: (0, 0)
    return pl.pallas_call(
        functools.partial(query_kernel, tenants),
        grid_spec=pltpu.PrefetchScalarGridSpec(
            num_scalar_prefetch=2,
            grid=(1,),
            in_specs=[
                pl.BlockSpec(array.shape, whole)
                for array in (one, two, own, other, raw, cosine, sine)
            ],
            out_specs=pl.BlockSpec(raw.shape, whole),
        ),
        out_shape=jax.ShapeDtypeStruct(raw.shape, jnp.bfloat16),
        compiler_params=pltpu.CompilerParams(vmem_limit_bytes=VMEM_LIMIT),
        name="query_rows",
    )(device, lengths, one, two, own, other, raw, cosine, sine)


def attend_kernel(
    tenants,
    device_ref,
    length_ref,
    q_ref,
    k4,
    k2,
    k31,
    k0,
    v4,
    v2,
    v31,
    v0,
    out_ref,
    keys,
    values,
    scores,
    peaks,
    totals,
    mixed,
):
    width = HEAD_WIDTH
    tokens = q_ref.shape[0]
    heads = q_ref.shape[1] // width
    behind = LONGEST_PROMPT * tokens
    chunk = scores.shape[2]
    rows = heads * TILE
    factor = HEAD_WIDTH ** (-0.5) * math.log2(math.e)
    base = (device_ref[0] - LONGEST_PROMPT) * tokens

    for target, four, two, odd, own in ((keys, k4, k2, k31, k0), (values, v4, v2, v31, v0)):
        target[:tokens, :] = four[...]
        target[tokens : 2 * tokens, :] = odd[tokens:, :]
        target[2 * tokens : 3 * tokens, :] = two[...]
        target[3 * tokens : 4 * tokens, :] = odd[:tokens, :]
        target[4 * tokens :, :] = own[...]

    def start_of(index):
        start = 0
        end = 0
        for t in range(tenants):
            end = end + length_ref[t]
            start = jnp.where(index >= end, end, start)
        return start

    for tile in range(tokens // TILE):
        at = slice(tile * TILE, (tile + 1) * TILE)
        begin = behind + tile * TILE
        low = start_of(base + begin) - base
        high = start_of(base + begin + TILE - 1) - base
        first = low // chunk
        last = (begin + TILE + chunk - 1) // chunk
        query = jnp.concatenate(
            [q_ref[at, head * width : (head + 1) * width] for head in range(heads)], axis=0
        )
        mine = begin + lax.broadcasted_iota(jnp.int32, (TILE, 1), 0)
        _, start = tenant_at(length_ref, tenants, base + mine)
        start = start - base
        peaks[...] = jnp.full((rows, width), -jnp.inf, jnp.float32)

        def score(c, carry, begin=begin, high=high, query=query, mine=mine, start=start):
            key = keys[pl.ds(pl.multiple_of(c * chunk, chunk), chunk), :]
            raw = lax.dot_general(
                query, key, (((1,), (1,)), ((), ())), preferred_element_type=jnp.float32
            )
            edge = (c * chunk < high) | ((c + 1) * chunk > begin + 1)

            def keep(now):
                scores[c] = now
                best = peaks[...]
                for piece in range(chunk // width):
                    best = jnp.maximum(best, now[:, piece * width : (piece + 1) * width])
                peaks[...] = best

            @pl.when(edge)
            def _():
                place = c * chunk + lax.broadcasted_iota(jnp.int32, (TILE, chunk), 1)
                allowed = (place >= start) & (place <= mine)
                keep(
                    jnp.where(
                        allowed[None], raw.reshape(heads, TILE, chunk), -jnp.inf
                    ).reshape(rows, chunk)
                )

            @pl.when(jnp.logical_not(edge))
            def _():
                keep(raw)

            return carry

        lax.fori_loop(first, last, score, 0)
        peak = jnp.max(peaks[...], axis=1, keepdims=True)
        totals[...] = jnp.zeros((rows, width), jnp.float32)
        mixed[...] = jnp.zeros((rows, width), jnp.float32)

        def mix(c, carry, peak=peak):
            weights = jnp.exp2((scores[c] - peak) * factor)
            total = totals[...]
            for piece in range(chunk // width):
                total = total + weights[:, piece * width : (piece + 1) * width]
            totals[...] = total
            mixed[...] += jnp.dot(
                weights.astype(jnp.bfloat16),
                values[pl.ds(pl.multiple_of(c * chunk, chunk), chunk), :],
                preferred_element_type=jnp.float32,
            )
            return carry

        lax.fori_loop(first, last, mix, 0)
        total = jnp.sum(totals[...], axis=1, keepdims=True)
        result = (mixed[...] / total).astype(jnp.bfloat16)
        for head in range(heads):
            out_ref[at, head * width : (head + 1) * width] = result[
                head * TILE : (head + 1) * TILE, :
            ]


def attend(device, lengths, query, keys, values):
    tenants = lengths.shape[0]
    tokens, cols = query.shape
    groups = keys[0].shape[1] // HEAD_WIDTH
    group_cols = cols // groups
    heads = group_cols // HEAD_WIDTH
    rows = heads * TILE
    span = (LONGEST_PROMPT + 1) * tokens
    by_group = lambda g, *_: (0, g)
    return pl.pallas_call(
        functools.partial(attend_kernel, tenants),
        grid_spec=pltpu.PrefetchScalarGridSpec(
            num_scalar_prefetch=2,
            grid=(groups,),
            in_specs=[pl.BlockSpec((tokens, group_cols), by_group)]
            + [pl.BlockSpec((array.shape[0], HEAD_WIDTH), by_group) for array in keys + values],
            out_specs=pl.BlockSpec((tokens, group_cols), by_group),
            scratch_shapes=[
                pltpu.VMEM((span, HEAD_WIDTH), jnp.bfloat16),
                pltpu.VMEM((span, HEAD_WIDTH), jnp.bfloat16),
                pltpu.VMEM((span // CHUNK, rows, CHUNK), jnp.float32),
                pltpu.VMEM((rows, HEAD_WIDTH), jnp.float32),
                pltpu.VMEM((rows, HEAD_WIDTH), jnp.float32),
                pltpu.VMEM((rows, HEAD_WIDTH), jnp.float32),
            ],
        ),
        out_shape=jax.ShapeDtypeStruct((tokens, cols), jnp.bfloat16),
        compiler_params=pltpu.CompilerParams(vmem_limit_bytes=VMEM_LIMIT),
        name="attention",
    )(device, lengths, query, *keys, *values)


def after(value, *others):
    return lax.optimization_barrier((value,) + others)[0]


def swap_cores(x):
    peers = lax.axis_size("tok")
    return lax.ppermute(x, "tok", [(i, i ^ 1) for i in range(peers)])


def from_behind(x, by):
    peers = lax.axis_size("tok")
    return lax.ppermute(x, "tok", [(i, i + by) for i in range(peers - by)])


def gather_behind(own, core):
    two = from_behind(own, 2)
    four = from_behind(own, 4)
    sent = jnp.where(
        core == 0, jnp.concatenate([own, two], axis=0), jnp.concatenate([two, four], axis=0)
    )
    return [four, two, swap_cores(sent), own]


def chip_orders():
    peers = lax.axis_size("tok")
    bits = [1 << b for b in range(1, (peers - 1).bit_length())]
    turn = len(bits) // 2
    orders = (bits, bits[turn:] + bits[:turn])
    return [
        [(i, i ^ orders[i % 2][step]) for i in range(peers)] for step in range(len(bits))
    ]


def body(
    layer_input,
    input_norm_gain,
    query_weight,
    key_weight,
    value_weight,
    query_down_maps,
    value_down_maps,
    query_up_maps,
    value_up_maps,
    tenant_prompt_length,
    tenant_adapter_id,
    adapter_storage_slot,
):
    tok_rows = layer_input.shape[0]
    axis_device = lax.axis_index("tok")
    core = axis_device % 2
    device = axis_device.reshape(1)
    lengths = tenant_prompt_length
    first, second = pick(
        tenant_adapter_id,
        adapter_storage_slot,
        device,
        query_down_maps,
        value_down_maps,
        query_up_maps,
        value_up_maps,
    )
    orders = chip_orders()
    sum_a = first[0] + swap_cores(first[1])
    sum_b = second[0] + swap_cores(second[1])
    indices = axis_device * tok_rows + jnp.arange(tok_rows, dtype=jnp.int32)
    cosine, sine = rotary_tables(positions_of(lengths, indices))
    key, raw_value, raw_query, share = project(
        lax.axis_index("mlp").reshape(1),
        layer_input,
        after(input_norm_gain[None, :], sum_a),
        key_weight,
        value_weight,
        query_weight,
        cosine,
        sine,
        lax.axis_size("mlp"),
    )
    for pairs in orders:
        sum_a = sum_a + lax.ppermute(sum_a, "tok", pairs)
    other_a = swap_cores(sum_a)
    for pairs in orders:
        sum_b = sum_b + lax.ppermute(sum_b, "tok", pairs)
    other_b = swap_cores(sum_b)
    keys = gather_behind(key, core)

    part = shrink(device, lengths, sum_a, other_a, share)
    levels = (lax.axis_size("mlp") - 1).bit_length()
    for level in range(levels):
        pairs = [(i, i ^ (1 << level)) for i in range(lax.axis_size("mlp"))]
        got = lax.ppermute(part, "mlp", pairs)
        if level + 1 < levels:
            part = part + got
    value = finish_value(device, lengths, part, got, sum_a, other_a, raw_value)
    values = gather_behind(value, core)
    query = finish_query(
        device, lengths, part, got, sum_b, other_b, raw_query, cosine, sine
    )
    return attend(device, lengths, query, keys, values)


def solution(mesh):
    placed = (
        P("tok", None),
        P(),
        P(None, "mlp"),
        P(None, "mlp"),
        P(None, "mlp"),
        P("tok", None, "mlp"),
        P("tok", None, "mlp"),
        P("tok", None, "mlp"),
        P("tok", None, "mlp"),
        P(),
        P(),
        P(),
    )
    return jax.shard_map(
        body, mesh=mesh, in_specs=placed, out_specs=P("tok", "mlp"), check_vma=False
    )
```

```python
import functools
import math

import jax
import jax.numpy as jnp
from jax import lax
from jax.experimental import pallas as pl
from jax.experimental.pallas import tpu as pltpu
from jax.sharding import PartitionSpec as P

HEAD_WIDTH = 128
ADAPTER_RANK = 16
LONGEST_PROMPT = 4
NORM_EPS = 1e-05
ROPE_BASE = 500000.0
ADAPTER_SCALE = 0.5
MIB = 1024 * 1024
TILE = 256
SLOT = 256


def positions_of(tenant_prompt_length, indices):
    prompt_ends = jnp.cumsum(tenant_prompt_length)
    passed = jnp.where(indices[:, None] >= prompt_ends[None, :], prompt_ends[None, :], 0)
    return indices - jnp.max(passed, axis=1)


def rotary_tables(positions):
    half_width = HEAD_WIDTH // 2
    exponent = jnp.arange(half_width).astype(jnp.float32) * (2.0 / HEAD_WIDTH)
    inverse = jnp.exp(-exponent * jnp.log(jnp.float32(ROPE_BASE)))
    angles = positions.astype(jnp.float32)[:, None] * inverse[None, :]
    cosine = jnp.cos(angles)
    sine = jnp.sin(angles)
    return jnp.concatenate([cosine, cosine], axis=1), jnp.concatenate([-sine, sine], axis=1)


def rope(x, cosine, sine):
    half = HEAD_WIDTH // 2
    swapped = jnp.concatenate([x[:, half:], x[:, :half]], axis=1)
    return x * cosine + swapped * sine


HERE = pl.BlockSpec(memory_space=pltpu.VMEM)
SCALARS = pl.BlockSpec(memory_space=pltpu.SMEM)
AWAY = pl.BlockSpec(memory_space=pltpu.HBM)


def kernel_call(kernel, name, mib, in_specs, out_shape, scratch_shapes=(), flops=0, bytes_accessed=0):
    return pl.pallas_call(
        kernel,
        in_specs=in_specs,
        out_specs=jax.tree.map(lambda _: HERE, out_shape),
        out_shape=out_shape,
        scratch_shapes=scratch_shapes,
        compiler_params=pltpu.CompilerParams(vmem_limit_bytes=mib * MIB),
        cost_estimate=pl.CostEstimate(
            flops=flops, bytes_accessed=bytes_accessed, transcendentals=0
        ),
        name=name,
    )


HEADER = 3


def pick_kernel(tenants, meta_ref, qd, vd, qu, vu, *refs):
    *outs, sems = refs
    device = meta_ref[0]
    core = lax.rem(device, 2)
    rank = ADAPTER_RANK
    held, _, wide = qd.shape
    narrow = vu.shape[2]
    count = tenants // 2
    ids = HEADER + tenants
    slots = ids + tenants
    jobs = []
    for side in range(2):
        half = core if side == 0 else 1 - core
        for t in range(count):
            slot = meta_ref[slots + meta_ref[ids + half * count + t]] - device * held
            here = (slot >= 0) & (slot < held)
            jobs.append((side, t, jnp.clip(slot, 0, held - 1), here))

    def copies(side, t, slot):
        first, second = outs[side], outs[2 + side]
        top = pl.ds(2 * t * rank, rank)
        low = pl.ds((2 * t + 1) * rank, rank)
        pairs = (
            (qd.at[slot], first.at[top, pl.ds(0, wide)]),
            (vd.at[slot], first.at[low, pl.ds(0, wide)]),
            (vu.at[slot], first.at[top, pl.ds(wide, narrow)]),
            (qu.at[slot], second.at[pl.ds(t * rank, rank), :]),
        )
        return [
            pltpu.make_async_copy(source, target, sems.at[side * count + t, number])
            for number, (source, target) in enumerate(pairs)
        ]

    for side, t, slot, here in jobs:

        @pl.when(here)
        def _(side=side, t=t, slot=slot):
            for copy in copies(side, t, slot):
                copy.start()

    for side, t, slot, here in jobs:
        first, second = outs[side], outs[2 + side]
        top, low, end = 2 * t * rank, (2 * t + 1) * rank, 2 * (t + 1) * rank
        first[low:end, wide:] = jnp.zeros((rank, narrow), jnp.bfloat16)

        @pl.when(jnp.logical_not(here))
        def _(first=first, second=second, t=t, top=top, low=low, end=end):
            first[top:low, :] = jnp.zeros((rank, wide + narrow), jnp.bfloat16)
            first[low:end, :wide] = jnp.zeros((rank, wide), jnp.bfloat16)
            second[t * rank : (t + 1) * rank, :] = jnp.zeros((rank, wide), jnp.bfloat16)

    for side, t, slot, here in jobs:

        @pl.when(here)
        def _(side=side, t=t, slot=slot):
            for copy in copies(side, t, slot):
                copy.wait()


def pick(tenants, meta, qd, vd, qu, vu):
    held, rank, wide = qd.shape
    narrow = vu.shape[2]
    rows = tenants * rank
    shapes = ((rows, wide + narrow),) * 2 + ((rows // 2, wide),) * 2
    maps = [pltpu.with_memory_space_constraint(x, pltpu.HBM) for x in (qd, vd, qu, vu)]
    return kernel_call(
        functools.partial(pick_kernel, tenants),
        "pick_adapters",
        4,
        [SCALARS] + [AWAY] * 4,
        [jax.ShapeDtypeStruct(shape, jnp.bfloat16) for shape in shapes],
        [pltpu.SemaphoreType.DMA((tenants, 4))],
    )(meta, *maps)


def kv_kernel(gain_ref, cos_ref, sin_ref, x, wk, wv, normed, key_ref, value_ref):
    rows = x.shape[0]
    width = HEAD_WIDTH
    step = rows // 4
    for top in range(0, rows, step):
        at = slice(top, top + step)
        wide = x[at, :].astype(jnp.float32)
        scale = lax.rsqrt(jnp.mean(wide * wide, axis=1, keepdims=True) + NORM_EPS)
        normed[at, :] = (wide * scale * gain_ref[...]).astype(jnp.bfloat16)
    raw = jnp.dot(normed[...], wk[...], preferred_element_type=jnp.float32)
    for head in range(key_ref.shape[1] // width):
        cols = slice(head * width, (head + 1) * width)
        key_ref[:, cols] = rope(raw[:, cols], cos_ref[...], sin_ref[...]).astype(jnp.bfloat16)
    value_ref[...] = jnp.dot(normed[...], wv[...], preferred_element_type=jnp.float32)


def project_kv(x, gain, wk, wv, cosine, sine):
    rows, model = x.shape
    cols = wk.shape[1]
    return kernel_call(
        kv_kernel,
        "norm_key_value",
        16,
        [HERE] * 6,
        [
            jax.ShapeDtypeStruct((rows, model), jnp.bfloat16),
            jax.ShapeDtypeStruct((rows, cols), jnp.bfloat16),
            jax.ShapeDtypeStruct((rows, cols), jnp.float32),
        ],
        flops=4 * rows * model * cols,
        bytes_accessed=4 * model * (rows + cols),
    )(gain, cosine, sine, x, wk, wv)


def query_projection_kernel(x, w, out_ref):
    tile = 256
    for at in range(0, w.shape[1], tile):
        out_ref[:, at : at + tile] = jnp.dot(
            x[...], w[:, at : at + tile], preferred_element_type=jnp.float32
        )


def project_query(normed, weight):
    rows, model = normed.shape
    cols = weight.shape[1]
    return kernel_call(
        query_projection_kernel,
        "query_projection",
        16,
        [HERE, HERE],
        jax.ShapeDtypeStruct((rows, cols), jnp.float32),
        flops=2 * rows * model * cols,
        bytes_accessed=2 * model * (rows + cols),
    )(normed, weight)


def tenant_at(meta_ref, tenants, index):
    tid = jnp.zeros(index.shape, jnp.int32)
    start = jnp.zeros(index.shape, jnp.int32)
    end = 0
    for t in range(tenants):
        end = end + meta_ref[HEADER + t]
        past = index >= end
        tid = jnp.where(past, t + 1, tid)
        start = jnp.where(past, end, start)
    return tid, start


def shrink_kernel(tenants, shares, meta_ref, own_ref, other_ref, x, out_ref):
    contract = (((1,), (1,)), ((), ()))
    tokens, model = x.shape
    kept = model // shares
    part = x[:, pl.ds(pl.multiple_of(meta_ref[1] * kept, kept), kept)]
    rows = 2 * ADAPTER_RANK
    count = tenants // 2
    core = lax.rem(meta_ref[0], 2)
    index = meta_ref[0] * tokens + lax.broadcasted_iota(jnp.int32, (1, tokens), 1)
    tid, _ = tenant_at(meta_ref, tenants, index)
    total = jnp.zeros((rows, tokens), jnp.float32)
    for ref, half in ((own_ref, core), (other_ref, 1 - core)):
        wide = lax.dot_general(ref[:, :kept], part, contract, preferred_element_type=jnp.float32)
        for t in range(count):
            total = total + jnp.where(
                tid == half * count + t, wide[t * rows : (t + 1) * rows, :], 0.0
            )
    out_ref[...] = total


def shrink(tenants, shares, meta, own, other, normed):
    return kernel_call(
        functools.partial(shrink_kernel, tenants, shares),
        "shrink_share",
        8,
        [SCALARS, HERE, HERE, HERE],
        jax.ShapeDtypeStruct((2 * ADAPTER_RANK, normed.shape[0]), jnp.float32),
    )(meta, own, other, normed)


def spread_tenants(tenants, parts, rows, meta_ref):
    parts = [part[rows, :] for part in parts]
    while len(parts) > 1:
        parts = [parts[i] + parts[i + 1] for i in range(0, len(parts), 2)]
    shrunk = parts[0]
    rank, tokens = shrunk.shape
    lanes = tenants * rank
    lane = lax.broadcasted_iota(jnp.int32, (rank, lanes), 1)
    repeat = (lane % rank == lax.broadcasted_iota(jnp.int32, (rank, lanes), 0)).astype(
        jnp.bfloat16
    )
    wide = lax.dot_general(
        shrunk.astype(jnp.bfloat16),
        repeat,
        (((0,), (0,)), ((), ())),
        preferred_element_type=jnp.float32,
    )
    index = meta_ref[0] * tokens + lax.broadcasted_iota(jnp.int32, (tokens, 1), 0)
    tid, _ = tenant_at(meta_ref, tenants, index)
    owner = lax.broadcasted_iota(jnp.int32, (1, lanes), 1) // rank
    return jnp.where(owner == tid, wide, 0.0).astype(jnp.bfloat16)


def value_kernel(tenants, shares, meta_ref, *refs):
    parts = refs[:shares]
    own_ref, other_ref, raw_ref, out_ref = refs[shares:]
    side = own_ref.shape[1] - raw_ref.shape[1]
    rank = ADAPTER_RANK
    spread = spread_tenants(tenants, parts, slice(rank, 2 * rank), meta_ref)
    even = lax.rem(meta_ref[0], 2) == 0
    own, other = (
        jnp.concatenate(
            [ref[top : top + rank, side:] for top in range(0, ref.shape[0], 2 * rank)], axis=0
        )
        for ref in (own_ref, other_ref)
    )
    up = jnp.concatenate([jnp.where(even, own, other), jnp.where(even, other, own)], axis=0)
    delta = jnp.dot(spread, up, preferred_element_type=jnp.float32)
    out_ref[...] = (raw_ref[...] + ADAPTER_SCALE * delta).astype(jnp.bfloat16)


def finish_value(tenants, meta, parts, own, other, raw):
    return kernel_call(
        functools.partial(value_kernel, tenants, len(parts)),
        "value_rows",
        5,
        [SCALARS] + [HERE] * (len(parts) + 3),
        jax.ShapeDtypeStruct(raw.shape, jnp.bfloat16),
    )(meta, *parts, own, other, raw)


def query_kernel(tenants, shares, meta_ref, *refs):
    rank = ADAPTER_RANK
    parts = refs[:shares]
    own_ref, other_ref, raw_ref, cos_ref, sin_ref, out_ref = refs[shares:]
    spread = spread_tenants(tenants, parts, slice(0, rank), meta_ref)
    even = lax.rem(meta_ref[0], 2) == 0
    own, other = own_ref[...], other_ref[...]
    up = jnp.concatenate([jnp.where(even, own, other), jnp.where(even, other, own)], axis=0)
    for top in range(0, raw_ref.shape[1], 2 * HEAD_WIDTH):
        delta = jnp.dot(
            spread, up[:, top : top + 2 * HEAD_WIDTH], preferred_element_type=jnp.float32
        )
        for head in range(2):
            local = slice(head * HEAD_WIDTH, (head + 1) * HEAD_WIDTH)
            cols = slice(top + head * HEAD_WIDTH, top + (head + 1) * HEAD_WIDTH)
            row = raw_ref[:, cols] + ADAPTER_SCALE * delta[:, local]
            out_ref[:, cols] = rope(row, cos_ref[...], sin_ref[...]).astype(jnp.bfloat16)


def finish_query(tenants, meta, parts, own, other, raw, cosine, sine):
    return kernel_call(
        functools.partial(query_kernel, tenants, len(parts)),
        "query_rows",
        8,
        [SCALARS] + [HERE] * (len(parts) + 5),
        jax.ShapeDtypeStruct(raw.shape, jnp.bfloat16),
    )(meta, *parts, own, other, raw, cosine, sine)


def attend_kernel(
    tenants, meta_ref, q_ref, k4, k2, k31, k0, v4, v2, v31, v0, out_ref, keys, values, scores, bias, peaks, totals, mixed
):
    width = HEAD_WIDTH
    tokens = q_ref.shape[0]
    all_heads = q_ref.shape[1] // width
    heads = q_ref.shape[1] // k0.shape[1]
    behind = LONGEST_PROMPT * tokens
    slots = behind // SLOT
    factor = HEAD_WIDTH ** (-0.5) * math.log2(math.e)
    base = (meta_ref[0] - LONGEST_PROMPT) * tokens

    for target, four, two, odd, own in ((keys, k4, k2, k31, k0), (values, v4, v2, v31, v0)):
        target[:tokens, :] = four[...]
        target[tokens : 2 * tokens, :] = odd[tokens:, :]
        target[2 * tokens : 3 * tokens, :] = two[...]
        target[3 * tokens : 4 * tokens, :] = odd[:tokens, :]
        target[4 * tokens :, :] = own[...]

    def start_of(index):
        start = 0
        end = 0
        for t in range(tenants):
            end = end + meta_ref[HEADER + t]
            start = jnp.where(index >= end, end, start)
        return start - base

    mine = behind + lax.broadcasted_iota(jnp.int32, (tokens, 1), 0)
    _, start = tenant_at(meta_ref, tenants, base + mine)
    start = start - base
    subs = []
    for head in range(all_heads):
        group = head // heads
        subs.append(
            (
                slice(head * TILE, (head + 1) * TILE),
                slice(head * width, (head + 1) * width),
                slice(group * width, (group + 1) * width),
            )
        )

    for tile in range(tokens // TILE):
        top = slice(tile * TILE, (tile + 1) * TILE)
        begin = behind + tile * TILE
        low = start_of(base + begin)
        high = start_of(base + begin + TILE - 1)
        first = jnp.minimum(low // SLOT, slots)
        odd = lax.rem(first, 2) == 1
        own_slots = (tile + 1) * TILE // SLOT

        def columns(slot, count):
            return pl.ds(pl.multiple_of(slot * SLOT, SLOT), count * SLOT)

        def score(slot, count, masked, fresh=False, top=top):
            at_keys = columns(slot, count)
            if masked:
                place = slot * SLOT + lax.broadcasted_iota(jnp.int32, (TILE, count * SLOT), 1)
                seen = (place >= start[top]) & (place <= mine[top])
                bias[:, : count * SLOT] = jnp.where(seen, 0.0, -jnp.inf)
            for at, head, group in subs:
                raw = lax.dot_general(
                    q_ref[top, head],
                    keys[at_keys, group],
                    (((1,), (1,)), ((), ())),
                    preferred_element_type=jnp.float32,
                )
                best = None if fresh else peaks[at, :]
                for piece in range(count * SLOT // width):
                    cols = slice(piece * width, (piece + 1) * width)
                    part = raw[:, cols] * factor
                    if masked:
                        part = part + bias[:, cols]
                    inner = piece * width % SLOT
                    scores[slot + piece * width // SLOT, at, inner : inner + width] = part
                    best = part if best is None else jnp.maximum(best, part)
                peaks[at, :] = best

        def mix(slot, count, fresh=False):
            at_values = columns(slot, count)
            for at, _, group in subs:
                peak = peaks[at, :]
                total = None if fresh else totals[at, :]
                probs = []
                for piece in range(count * SLOT // width):
                    inner = piece * width % SLOT
                    weights = jnp.exp2(
                        scores[slot + piece * width // SLOT, at, inner : inner + width] - peak
                    )
                    total = weights if total is None else total + weights
                    probs.append(weights.astype(jnp.bfloat16))
                totals[at, :] = total
                part = jnp.dot(
                    jnp.concatenate(probs, axis=1),
                    values[at_values, group],
                    preferred_element_type=jnp.float32,
                )
                if fresh:
                    mixed[at, :] = part
                else:
                    mixed[at, :] += part

        def pair(c, carry, high=high, score=score):
            edge = c * 2 * SLOT < high
            pl.when(edge)(lambda: score(2 * c, 2, True))
            pl.when(jnp.logical_not(edge))(lambda: score(2 * c, 2, False))
            return carry

        def mix_pair(c, carry, mix=mix):
            mix(2 * c, 2)
            return carry

        score(slots, own_slots, True, fresh=True)
        pl.when(odd)(lambda: score(first, 1, True))
        lax.fori_loop((first + 1) // 2, slots // 2, pair, 0)
        for at, _, _ in subs:
            peaks[at, :] = jnp.broadcast_to(
                jnp.max(peaks[at, :], axis=1, keepdims=True), (TILE, width)
            )
        mix(slots, own_slots, fresh=True)
        pl.when(odd)(lambda: mix(first, 1))
        lax.fori_loop((first + 1) // 2, slots // 2, mix_pair, 0)
        for at, head, _ in subs:
            total = jnp.sum(totals[at, :], axis=1, keepdims=True)
            out_ref[top, head] = (mixed[at, :] / total).astype(jnp.bfloat16)


def attend(tenants, meta, query, keys, values):
    tokens, cols = query.shape
    kv_cols = keys[0].shape[1]
    rows = cols // HEAD_WIDTH * TILE
    span = (LONGEST_PROMPT + 1) * tokens
    return kernel_call(
        functools.partial(attend_kernel, tenants),
        "attention",
        34,
        [SCALARS] + [HERE] * (1 + len(keys) + len(values)),
        jax.ShapeDtypeStruct((tokens, cols), jnp.bfloat16),
        [
            pltpu.VMEM((span, kv_cols), jnp.bfloat16),
            pltpu.VMEM((span, kv_cols), jnp.bfloat16),
            pltpu.VMEM((span // SLOT, rows, SLOT), jnp.float32),
            pltpu.VMEM((TILE, 2 * SLOT), jnp.float32),
            pltpu.VMEM((rows, HEAD_WIDTH), jnp.float32),
            pltpu.VMEM((rows, HEAD_WIDTH), jnp.float32),
            pltpu.VMEM((rows, HEAD_WIDTH), jnp.float32),
        ],
    )(meta, query, *keys, *values)


def after(value, *others):
    return lax.optimization_barrier((value,) + others)[0]


def swap_cores(x):
    peers = lax.axis_size("tok")
    return lax.ppermute(x, "tok", [(i, i ^ 1) for i in range(peers)])


def from_behind(x, by):
    peers = lax.axis_size("tok")
    return lax.ppermute(x, "tok", [(i, i + by) for i in range(peers - by)])


def gather_behind(own, core):
    two = from_behind(own, 2)
    four = from_behind(own, 4)
    sent = jnp.where(
        core == 0, jnp.concatenate([own, two], axis=0), jnp.concatenate([two, four], axis=0)
    )
    return [four, two, swap_cores(sent), own]


def chip_orders():
    peers = lax.axis_size("tok")
    bits = [1 << b for b in range(1, (peers - 1).bit_length())]
    turn = len(bits) // 2
    orders = (bits, bits[turn:] + bits[:turn])
    return [
        [(i, i ^ orders[i % 2][step]) for i in range(peers)] for step in range(len(bits))
    ]


def body(
    layer_input,
    input_norm_gain,
    query_weight,
    key_weight,
    value_weight,
    query_down_maps,
    value_down_maps,
    query_up_maps,
    value_up_maps,
    tenant_prompt_length,
    tenant_adapter_id,
    adapter_storage_slot,
):
    tok_rows = layer_input.shape[0]
    device = lax.axis_index("tok")
    shares = lax.axis_size("mlp")
    core = device % 2
    lengths = tenant_prompt_length
    tenants = lengths.shape[0]
    places = jnp.stack([device, lax.axis_index("mlp"), jnp.int32(tenants)])
    meta = jnp.concatenate([places, lengths, tenant_adapter_id, adapter_storage_slot])
    first, first_sent, second, second_sent = pick(
        tenants, meta, query_down_maps, value_down_maps, query_up_maps, value_up_maps
    )
    orders = chip_orders()
    steps = len(orders)
    indices = device * tok_rows + jnp.arange(tok_rows, dtype=jnp.int32)
    cosine, sine = rotary_tables(positions_of(lengths, after(indices, first)))

    def shared(part):
        parts = [part]
        for bit in range(1, shares):
            parts.append(lax.ppermute(part, "mlp", [(i, i ^ bit) for i in range(shares)]))
        return parts

    sum_a = first + swap_cores(first_sent)
    got_a = lax.ppermute(sum_a, "tok", orders[0])
    gain, sum_a = lax.optimization_barrier((input_norm_gain[None, :], sum_a))
    normed, key, raw_value = project_kv(layer_input, gain, key_weight, value_weight, cosine, sine)
    sum_b = second + swap_cores(second_sent)
    got_a, key, sum_b = lax.optimization_barrier((got_a, key, sum_b))
    for step in range(1, steps):
        sum_a = sum_a + got_a
        got_a = lax.ppermute(sum_a, "tok", orders[step])
    normed, sum_a = lax.optimization_barrier((normed, sum_a))
    raw_query = project_query(normed, query_weight)
    got_a, raw_query = lax.optimization_barrier((got_a, raw_query))
    sum_a = sum_a + got_a
    other_a = swap_cores(sum_a)
    sum_b, key = lax.optimization_barrier((sum_b, key, sum_a))[:2]
    got_b = lax.ppermute(sum_b, "tok", orders[0])
    parts = shared(shrink(tenants, shares, meta, sum_a, other_a, normed))
    value = finish_value(tenants, meta, parts, sum_a, other_a, raw_value)
    for step in range(1, steps):
        sum_b = sum_b + got_b
        got_b = lax.ppermute(sum_b, "tok", orders[step])
    sum_b = sum_b + got_b
    other_b = swap_cores(sum_b)
    keys = gather_behind(key, core)
    values = gather_behind(value, core)
    query = finish_query(tenants, meta, parts, sum_b, other_b, raw_query, cosine, sine)
    return attend(tenants, meta, query, keys, values)


def solution(mesh):
    placed = (
        P("tok", None),
        P(),
        P(None, "mlp"),
        P(None, "mlp"),
        P(None, "mlp"),
        P("tok", None, "mlp"),
        P("tok", None, "mlp"),
        P("tok", None, "mlp"),
        P("tok", None, "mlp"),
        P(),
        P(),
        P(),
    )
    return jax.shard_map(
        body, mesh=mesh, in_specs=placed, out_specs=P("tok", "mlp"), check_vma=False
    )
```

```python
import functools
import math

import jax
import jax.numpy as jnp
from jax import lax
from jax.experimental import pallas as pl
from jax.experimental.pallas import tpu as pltpu
from jax.sharding import PartitionSpec as P

HEAD_WIDTH = 128
ADAPTER_RANK = 16
LONGEST_PROMPT = 4
NORM_EPS = 1e-05
ROPE_BASE = 500000.0
ADAPTER_SCALE = 0.5
MIB = 1024 * 1024
TILE = 256
SLOT = 256
EARLY_TILES = 1


def positions_of(tenant_prompt_length, indices):
    prompt_ends = jnp.cumsum(tenant_prompt_length)
    passed = jnp.where(indices[:, None] >= prompt_ends[None, :], prompt_ends[None, :], 0)
    return indices - jnp.max(passed, axis=1)


def rotary_tables(positions):
    half_width = HEAD_WIDTH // 2
    exponent = jnp.arange(half_width).astype(jnp.float32) * (2.0 / HEAD_WIDTH)
    inverse = jnp.exp(-exponent * jnp.log(jnp.float32(ROPE_BASE)))
    angles = positions.astype(jnp.float32)[:, None] * inverse[None, :]
    cosine = jnp.cos(angles)
    sine = jnp.sin(angles)
    return jnp.concatenate([cosine, cosine], axis=1), jnp.concatenate([-sine, sine], axis=1)


def rope(x, cosine, sine):
    half = HEAD_WIDTH // 2
    swapped = jnp.concatenate([x[:, half:], x[:, :half]], axis=1)
    return x * cosine + swapped * sine


HERE = pl.BlockSpec(memory_space=pltpu.VMEM)
SCALARS = pl.BlockSpec(memory_space=pltpu.SMEM)
AWAY = pl.BlockSpec(memory_space=pltpu.HBM)


def kernel_call(kernel, name, mib, in_specs, out_shape, scratch_shapes=(), flops=0, bytes_accessed=0):
    return pl.pallas_call(
        kernel,
        in_specs=in_specs,
        out_specs=jax.tree.map(lambda _: HERE, out_shape),
        out_shape=out_shape,
        scratch_shapes=scratch_shapes,
        compiler_params=pltpu.CompilerParams(vmem_limit_bytes=mib * MIB),
        cost_estimate=pl.CostEstimate(
            flops=flops, bytes_accessed=bytes_accessed, transcendentals=0
        ),
        name=name,
    )


HEADER = 3


def pick_kernel(tenants, meta_ref, qd, vd, qu, vu, *refs):
    *outs, sems = refs
    device = meta_ref[0]
    core = lax.rem(device, 2)
    rank = ADAPTER_RANK
    held, _, wide = qd.shape
    narrow = vu.shape[2] // 2
    count = tenants // 2
    ids = HEADER + tenants
    slots = ids + tenants
    jobs = []
    for side in range(2):
        half = core if side == 0 else 1 - core
        for t in range(count):
            slot = meta_ref[slots + meta_ref[ids + half * count + t]] - device * held
            here = (slot >= 0) & (slot < held)
            jobs.append((side, t, jnp.clip(slot, 0, held - 1), here))

    def copies(side, t, slot):
        first, second = outs[side], outs[2 + side]
        top = pl.ds(2 * t * rank, rank)
        low = pl.ds((2 * t + 1) * rank, rank)
        pairs = (
            (qd.at[slot], first.at[top, pl.ds(0, wide)]),
            (vd.at[slot], first.at[low, pl.ds(0, wide)]),
            (vu.at[slot, :, pl.ds(0, narrow)], first.at[top, pl.ds(wide, narrow)]),
            (vu.at[slot, :, pl.ds(narrow, narrow)], first.at[low, pl.ds(wide, narrow)]),
            (qu.at[slot], second.at[pl.ds(t * rank, rank), :]),
        )
        return [
            pltpu.make_async_copy(source, target, sems.at[side * count + t, number])
            for number, (source, target) in enumerate(pairs)
        ]

    for side, t, slot, here in jobs:

        @pl.when(here)
        def _(side=side, t=t, slot=slot):
            for copy in copies(side, t, slot):
                copy.start()

    for side, t, slot, here in jobs:
        first, second = outs[side], outs[2 + side]

        @pl.when(jnp.logical_not(here))
        def _(first=first, second=second, t=t):
            first[2 * t * rank : 2 * (t + 1) * rank, :] = jnp.zeros(
                (2 * rank, wide + narrow), jnp.bfloat16
            )
            second[t * rank : (t + 1) * rank, :] = jnp.zeros((rank, wide), jnp.bfloat16)

    for side, t, slot, here in jobs:

        @pl.when(here)
        def _(side=side, t=t, slot=slot):
            for copy in copies(side, t, slot):
                copy.wait()


def pick(tenants, meta, qd, vd, qu, vu):
    held, rank, wide = qd.shape
    narrow = vu.shape[2] // 2
    rows = tenants * rank
    shapes = ((rows, wide + narrow),) * 2 + ((rows // 2, wide),) * 2
    maps = [pltpu.with_memory_space_constraint(x, pltpu.HBM) for x in (qd, vd, qu, vu)]
    return kernel_call(
        functools.partial(pick_kernel, tenants),
        "pick_adapters",
        4,
        [SCALARS] + [AWAY] * 4,
        [jax.ShapeDtypeStruct(shape, jnp.bfloat16) for shape in shapes],
        [pltpu.SemaphoreType.DMA((tenants, 5))],
    )(meta, *maps)


def kv_kernel(gain_ref, cos_ref, sin_ref, x, wk, wv, normed, key_ref, value_ref):
    rows = x.shape[0]
    width = HEAD_WIDTH
    step = rows // 4
    for top in range(0, rows, step):
        at = slice(top, top + step)
        wide = x[at, :].astype(jnp.float32)
        scale = lax.rsqrt(jnp.mean(wide * wide, axis=1, keepdims=True) + NORM_EPS)
        normed[at, :] = (wide * scale * gain_ref[...]).astype(jnp.bfloat16)
    raw = jnp.dot(normed[...], wk[...], preferred_element_type=jnp.float32)
    for head in range(key_ref.shape[1] // width):
        cols = slice(head * width, (head + 1) * width)
        key_ref[:, cols] = rope(raw[:, cols], cos_ref[...], sin_ref[...]).astype(jnp.bfloat16)
    value_ref[...] = jnp.dot(normed[...], wv[...], preferred_element_type=jnp.float32)


def project_kv(x, gain, wk, wv, cosine, sine):
    rows, model = x.shape
    cols = wk.shape[1]
    return kernel_call(
        kv_kernel,
        "norm_key_value",
        16,
        [HERE] * 6,
        [
            jax.ShapeDtypeStruct((rows, model), jnp.bfloat16),
            jax.ShapeDtypeStruct((rows, cols), jnp.bfloat16),
            jax.ShapeDtypeStruct((rows, cols), jnp.float32),
        ],
        flops=4 * rows * model * cols,
        bytes_accessed=4 * model * (rows + cols),
    )(gain, cosine, sine, x, wk, wv)


def query_projection_kernel(x, w, out_ref):
    tile = 256
    for at in range(0, w.shape[1], tile):
        out_ref[:, at : at + tile] = jnp.dot(
            x[...], w[:, at : at + tile], preferred_element_type=jnp.float32
        )


def project_query(normed, weight):
    rows, model = normed.shape
    cols = weight.shape[1]
    return kernel_call(
        query_projection_kernel,
        "query_projection",
        16,
        [HERE, HERE],
        jax.ShapeDtypeStruct((rows, cols), jnp.float32),
        flops=2 * rows * model * cols,
        bytes_accessed=2 * model * (rows + cols),
    )(normed, weight)


def tenant_at(meta_ref, tenants, index):
    tid = jnp.zeros(index.shape, jnp.int32)
    start = jnp.zeros(index.shape, jnp.int32)
    end = 0
    for t in range(tenants):
        end = end + meta_ref[HEADER + t]
        past = index >= end
        tid = jnp.where(past, t + 1, tid)
        start = jnp.where(past, end, start)
    return tid, start


def shrink_kernel(tenants, shares, meta_ref, own_ref, other_ref, x, out_ref):
    contract = (((1,), (1,)), ((), ()))
    tokens, model = x.shape
    kept = model // shares
    part = x[:, pl.ds(pl.multiple_of(meta_ref[1] * kept, kept), kept)]
    rows = 2 * ADAPTER_RANK
    count = tenants // 2
    core = lax.rem(meta_ref[0], 2)
    index = meta_ref[0] * tokens + lax.broadcasted_iota(jnp.int32, (1, tokens), 1)
    tid, _ = tenant_at(meta_ref, tenants, index)
    total = jnp.zeros((rows, tokens), jnp.float32)
    for ref, half in ((own_ref, core), (other_ref, 1 - core)):
        wide = lax.dot_general(ref[:, :kept], part, contract, preferred_element_type=jnp.float32)
        for t in range(count):
            total = total + jnp.where(
                tid == half * count + t, wide[t * rows : (t + 1) * rows, :], 0.0
            )
    out_ref[...] = total


def shrink(tenants, shares, meta, own, other, normed):
    return kernel_call(
        functools.partial(shrink_kernel, tenants, shares),
        "shrink_share",
        8,
        [SCALARS, HERE, HERE, HERE],
        jax.ShapeDtypeStruct((2 * ADAPTER_RANK, normed.shape[0]), jnp.float32),
    )(meta, own, other, normed)


def spread_tenants(tenants, parts, rows, meta_ref):
    parts = [part[rows, :] for part in parts]
    while len(parts) > 1:
        parts = [parts[i] + parts[i + 1] for i in range(0, len(parts), 2)]
    shrunk = parts[0]
    rank, tokens = shrunk.shape
    lanes = tenants * rank
    lane = lax.broadcasted_iota(jnp.int32, (rank, lanes), 1)
    repeat = (lane % rank == lax.broadcasted_iota(jnp.int32, (rank, lanes), 0)).astype(
        jnp.bfloat16
    )
    wide = lax.dot_general(
        shrunk.astype(jnp.bfloat16),
        repeat,
        (((0,), (0,)), ((), ())),
        preferred_element_type=jnp.float32,
    )
    index = meta_ref[0] * tokens + lax.broadcasted_iota(jnp.int32, (tokens, 1), 0)
    tid, _ = tenant_at(meta_ref, tenants, index)
    owner = lax.broadcasted_iota(jnp.int32, (1, lanes), 1) // rank
    return jnp.where(owner == tid, wide, 0.0).astype(jnp.bfloat16)


def value_kernel(tenants, shares, meta_ref, *refs):
    parts = refs[:shares]
    own_ref, other_ref, raw_ref, out_ref = refs[shares:]
    side = own_ref.shape[1] - raw_ref.shape[1] // 2
    rank = ADAPTER_RANK
    spread = spread_tenants(tenants, parts, slice(rank, 2 * rank), meta_ref)
    even = lax.rem(meta_ref[0], 2) == 0
    own, other = (
        jnp.concatenate(
            [
                jnp.concatenate(
                    [ref[top : top + rank, side:], ref[top + rank : top + 2 * rank, side:]], axis=1
                )
                for top in range(0, ref.shape[0], 2 * rank)
            ],
            axis=0,
        )
        for ref in (own_ref, other_ref)
    )
    up = jnp.concatenate([jnp.where(even, own, other), jnp.where(even, other, own)], axis=0)
    delta = jnp.dot(spread, up, preferred_element_type=jnp.float32)
    out_ref[...] = (raw_ref[...] + ADAPTER_SCALE * delta).astype(jnp.bfloat16)


def finish_value(tenants, meta, parts, own, other, raw):
    return kernel_call(
        functools.partial(value_kernel, tenants, len(parts)),
        "value_rows",
        5,
        [SCALARS] + [HERE] * (len(parts) + 3),
        jax.ShapeDtypeStruct(raw.shape, jnp.bfloat16),
    )(meta, *parts, own, other, raw)


def query_kernel(tenants, shares, meta_ref, *refs):
    rank = ADAPTER_RANK
    parts = refs[:shares]
    own_ref, other_ref, raw_ref, cos_ref, sin_ref, out_ref = refs[shares:]
    spread = spread_tenants(tenants, parts, slice(0, rank), meta_ref)
    even = lax.rem(meta_ref[0], 2) == 0
    own, other = own_ref[...], other_ref[...]
    up = jnp.concatenate([jnp.where(even, own, other), jnp.where(even, other, own)], axis=0)
    for top in range(0, raw_ref.shape[1], 2 * HEAD_WIDTH):
        delta = jnp.dot(
            spread, up[:, top : top + 2 * HEAD_WIDTH], preferred_element_type=jnp.float32
        )
        for head in range(2):
            local = slice(head * HEAD_WIDTH, (head + 1) * HEAD_WIDTH)
            cols = slice(top + head * HEAD_WIDTH, top + (head + 1) * HEAD_WIDTH)
            row = raw_ref[:, cols] + ADAPTER_SCALE * delta[:, local]
            out_ref[:, cols] = rope(row, cos_ref[...], sin_ref[...]).astype(jnp.bfloat16)


def finish_query(tenants, meta, parts, own, other, raw, cosine, sine):
    return kernel_call(
        functools.partial(query_kernel, tenants, len(parts)),
        "query_rows",
        8,
        [SCALARS] + [HERE] * (len(parts) + 5),
        jax.ShapeDtypeStruct(raw.shape, jnp.bfloat16),
    )(meta, *parts, own, other, raw, cosine, sine)


def tile_bounds(tenants, meta_ref, tokens):
    base = (meta_ref[0] - LONGEST_PROMPT) * tokens
    behind = LONGEST_PROMPT * tokens

    def start_of(index):
        start = 0
        end = 0
        for t in range(tenants):
            end = end + meta_ref[HEADER + t]
            start = jnp.where(index >= end, end, start)
        return start - base

    bounds = []
    for begin in range(behind, behind + tokens, TILE):
        low = start_of(base + begin)
        high = start_of(base + begin + TILE - 1)
        bounds.append((jnp.minimum(low // SLOT, behind // SLOT), high))
    return bounds


def line_up(target, four, two, odd, own):
    tokens = own.shape[0]
    target[:tokens, :] = four[...]
    target[tokens : 2 * tokens, :] = odd[tokens:, :]
    target[2 * tokens : 3 * tokens, :] = two[...]
    target[3 * tokens : 4 * tokens, :] = odd[:tokens, :]
    target[4 * tokens :, :] = own[...]


def head_rows(all_heads, groups):
    width = HEAD_WIDTH
    found = []
    for head in range(all_heads):
        group = head * groups // all_heads
        found.append(
            (
                slice(head * TILE, (head + 1) * TILE),
                slice(head * width, (head + 1) * width),
                slice(group * width, (group + 1) * width),
            )
        )
    return found


def weights_kernel(
    tenants, meta_ref, q_ref, k4, k2, k31, k0, probs, totals, keys, scores, bias, peaks
):
    width = HEAD_WIDTH
    tokens = q_ref.shape[0]
    behind = LONGEST_PROMPT * tokens
    slots = behind // SLOT
    factor = HEAD_WIDTH ** (-0.5) * math.log2(math.e)
    base = (meta_ref[0] - LONGEST_PROMPT) * tokens
    line_up(keys, k4, k2, k31, k0)
    mine = behind + lax.broadcasted_iota(jnp.int32, (tokens, 1), 0)
    _, start = tenant_at(meta_ref, tenants, base + mine)
    start = start - base
    subs = head_rows(q_ref.shape[1] // width, k0.shape[1] // width)
    bounds = tile_bounds(tenants, meta_ref, tokens)

    for tile, (first, high) in enumerate(bounds[:EARLY_TILES]):
        top = slice(tile * TILE, (tile + 1) * TILE)
        odd = lax.rem(first, 2) == 1
        own_slots = (tile + 1) * TILE // SLOT

        def score(slot, count, masked, fresh=False, top=top):
            at_keys = pl.ds(pl.multiple_of(slot * SLOT, SLOT), count * SLOT)
            if masked:
                place = slot * SLOT + lax.broadcasted_iota(jnp.int32, (TILE, count * SLOT), 1)
                seen = (place >= start[top]) & (place <= mine[top])
                bias[:, : count * SLOT] = jnp.where(seen, 0.0, -jnp.inf)
            for at, head, group in subs:
                raw = lax.dot_general(
                    q_ref[top, head],
                    keys[at_keys, group],
                    (((1,), (1,)), ((), ())),
                    preferred_element_type=jnp.float32,
                )
                best = None if fresh else peaks[at, :]
                for piece in range(count * SLOT // width):
                    cols = slice(piece * width, (piece + 1) * width)
                    part = raw[:, cols] * factor
                    if masked:
                        part = part + bias[:, cols]
                    inner = piece * width % SLOT
                    scores[slot + piece * width // SLOT, at, inner : inner + width] = part
                    best = part if best is None else jnp.maximum(best, part)
                peaks[at, :] = best

        def weigh(slot, count, fresh=False, tile=tile):
            for at, _, _ in subs:
                peak = peaks[at, :]
                total = None if fresh else totals[tile, at, :]
                for piece in range(count * SLOT // width):
                    inner = piece * width % SLOT
                    place = slot + piece * width // SLOT
                    weights = jnp.exp2(scores[place, at, inner : inner + width] - peak)
                    total = weights if total is None else total + weights
                    probs[tile, place, at, inner : inner + width] = weights.astype(jnp.bfloat16)
                totals[tile, at, :] = total

        def pair(c, carry, high=high, score=score):
            edge = c * 2 * SLOT < high
            pl.when(edge)(lambda: score(2 * c, 2, True))
            pl.when(jnp.logical_not(edge))(lambda: score(2 * c, 2, False))
            return carry

        def weigh_pair(c, carry, weigh=weigh):
            weigh(2 * c, 2)
            return carry

        score(slots, own_slots, True, fresh=True)
        pl.when(odd)(lambda: score(first, 1, True))
        lax.fori_loop((first + 1) // 2, slots // 2, pair, 0)
        for at, _, _ in subs:
            peaks[at, :] = jnp.broadcast_to(
                jnp.max(peaks[at, :], axis=1, keepdims=True), (TILE, width)
            )
        weigh(slots, own_slots, fresh=True)
        pl.when(odd)(lambda: weigh(first, 1))
        lax.fori_loop((first + 1) // 2, slots // 2, weigh_pair, 0)


def attention_weights(tenants, meta, query, keys):
    tokens, cols = query.shape
    kv_cols = keys[-1].shape[1]
    rows = cols // HEAD_WIDTH * TILE
    span = (LONGEST_PROMPT + 1) * tokens
    slots = span // SLOT
    tiles = EARLY_TILES
    return pl.pallas_call(
        functools.partial(weights_kernel, tenants),
        in_specs=[SCALARS] + [HERE] * (1 + len(keys)),
        out_specs=[HERE, HERE],
        out_shape=[
            pltpu.VMEM((tiles, slots, rows, SLOT), jnp.bfloat16),
            pltpu.VMEM((tiles, rows, HEAD_WIDTH), jnp.float32),
        ],
        scratch_shapes=[
            pltpu.VMEM((span, kv_cols), jnp.bfloat16),
            pltpu.VMEM((slots, rows, SLOT), jnp.float32),
            pltpu.VMEM((TILE, 2 * SLOT), jnp.float32),
            pltpu.VMEM((rows, HEAD_WIDTH), jnp.float32),
        ],
        compiler_params=pltpu.CompilerParams(vmem_limit_bytes=30 * MIB),
        name="attention_weights",
    )(meta, query, *keys)


def attend_kernel(
    tenants, meta_ref, q_ref, early, early_totals, k4, k2, k31, k0, v4, v2, v31, v0, out_ref,
    keys, values, scores, bias, peaks, totals, mixed,
):
    width = HEAD_WIDTH
    tokens = q_ref.shape[0]
    behind = LONGEST_PROMPT * tokens
    slots = behind // SLOT
    factor = HEAD_WIDTH ** (-0.5) * math.log2(math.e)
    base = (meta_ref[0] - LONGEST_PROMPT) * tokens
    line_up(keys, k4, k2, k31, k0)
    line_up(values, v4, v2, v31, v0)
    mine = behind + lax.broadcasted_iota(jnp.int32, (tokens, 1), 0)
    _, start = tenant_at(meta_ref, tenants, base + mine)
    start = start - base
    subs = head_rows(q_ref.shape[1] // width, k0.shape[1] // width)
    bounds = tile_bounds(tenants, meta_ref, tokens)

    for tile, (first, _) in enumerate(bounds[:EARLY_TILES]):
        top = slice(tile * TILE, (tile + 1) * TILE)

        def mix_early(slot, count, fresh=False, tile=tile):
            at_values = pl.ds(pl.multiple_of(slot * SLOT, SLOT), count * SLOT)
            for at, _, group in subs:
                part = jnp.dot(
                    jnp.concatenate(
                        [early[tile, slot + step, at, :] for step in range(count)], axis=1
                    ),
                    values[at_values, group],
                    preferred_element_type=jnp.float32,
                )
                if fresh:
                    mixed[at, :] = part
                else:
                    mixed[at, :] += part

        def early_pair(c, carry, mix_early=mix_early):
            mix_early(2 * c, 2)
            return carry

        mix_early(slots, (tile + 1) * TILE // SLOT, fresh=True)
        pl.when(lax.rem(first, 2) == 1)(lambda: mix_early(first, 1))
        lax.fori_loop((first + 1) // 2, slots // 2, early_pair, 0)
        for at, head, _ in subs:
            total = jnp.sum(early_totals[tile, at, :], axis=1, keepdims=True)
            out_ref[top, head] = (mixed[at, :] / total).astype(jnp.bfloat16)

    for tile in range(EARLY_TILES, tokens // TILE):
        top = slice(tile * TILE, (tile + 1) * TILE)
        first, high = bounds[tile]
        odd = lax.rem(first, 2) == 1
        own_slots = (tile + 1) * TILE // SLOT

        def columns(slot, count):
            return pl.ds(pl.multiple_of(slot * SLOT, SLOT), count * SLOT)

        def score(slot, count, masked, fresh=False, top=top):
            at_keys = columns(slot, count)
            if masked:
                place = slot * SLOT + lax.broadcasted_iota(jnp.int32, (TILE, count * SLOT), 1)
                seen = (place >= start[top]) & (place <= mine[top])
                bias[:, : count * SLOT] = jnp.where(seen, 0.0, -jnp.inf)
            for at, head, group in subs:
                raw = lax.dot_general(
                    q_ref[top, head],
                    keys[at_keys, group],
                    (((1,), (1,)), ((), ())),
                    preferred_element_type=jnp.float32,
                )
                best = None if fresh else peaks[at, :]
                for piece in range(count * SLOT // width):
                    cols = slice(piece * width, (piece + 1) * width)
                    part = raw[:, cols] * factor
                    if masked:
                        part = part + bias[:, cols]
                    inner = piece * width % SLOT
                    scores[slot + piece * width // SLOT, at, inner : inner + width] = part
                    best = part if best is None else jnp.maximum(best, part)
                peaks[at, :] = best

        def mix(slot, count, fresh=False):
            at_values = columns(slot, count)
            for at, _, group in subs:
                peak = peaks[at, :]
                total = None if fresh else totals[at, :]
                probs = []
                for piece in range(count * SLOT // width):
                    inner = piece * width % SLOT
                    weights = jnp.exp2(
                        scores[slot + piece * width // SLOT, at, inner : inner + width] - peak
                    )
                    total = weights if total is None else total + weights
                    probs.append(weights.astype(jnp.bfloat16))
                totals[at, :] = total
                part = jnp.dot(
                    jnp.concatenate(probs, axis=1),
                    values[at_values, group],
                    preferred_element_type=jnp.float32,
                )
                if fresh:
                    mixed[at, :] = part
                else:
                    mixed[at, :] += part

        def pair(c, carry, high=high, score=score):
            edge = c * 2 * SLOT < high
            pl.when(edge)(lambda: score(2 * c, 2, True))
            pl.when(jnp.logical_not(edge))(lambda: score(2 * c, 2, False))
            return carry

        def mix_pair(c, carry, mix=mix):
            mix(2 * c, 2)
            return carry

        score(slots, own_slots, True, fresh=True)
        pl.when(odd)(lambda: score(first, 1, True))
        lax.fori_loop((first + 1) // 2, slots // 2, pair, 0)
        for at, _, _ in subs:
            peaks[at, :] = jnp.broadcast_to(
                jnp.max(peaks[at, :], axis=1, keepdims=True), (TILE, width)
            )
        mix(slots, own_slots, fresh=True)
        pl.when(odd)(lambda: mix(first, 1))
        lax.fori_loop((first + 1) // 2, slots // 2, mix_pair, 0)
        for at, head, _ in subs:
            total = jnp.sum(totals[at, :], axis=1, keepdims=True)
            out_ref[top, head] = (mixed[at, :] / total).astype(jnp.bfloat16)


def attend(tenants, meta, query, early, early_totals, keys, values):
    tokens, cols = query.shape
    kv_cols = keys[-1].shape[1]
    rows = cols // HEAD_WIDTH * TILE
    span = (LONGEST_PROMPT + 1) * tokens
    return kernel_call(
        functools.partial(attend_kernel, tenants),
        "attention",
        36,
        [SCALARS] + [HERE] * (3 + len(keys) + len(values)),
        jax.ShapeDtypeStruct((tokens, cols), jnp.bfloat16),
        [
            pltpu.VMEM((span, kv_cols), jnp.bfloat16),
            pltpu.VMEM((span, kv_cols), jnp.bfloat16),
            pltpu.VMEM((span // SLOT, rows, SLOT), jnp.float32),
            pltpu.VMEM((TILE, 2 * SLOT), jnp.float32),
            pltpu.VMEM((rows, HEAD_WIDTH), jnp.float32),
            pltpu.VMEM((rows, HEAD_WIDTH), jnp.float32),
            pltpu.VMEM((rows, HEAD_WIDTH), jnp.float32),
        ],
    )(meta, query, early, early_totals, *keys, *values)


def after(value, *others):
    return lax.optimization_barrier((value,) + others)[0]


def swap_cores(x):
    peers = lax.axis_size("tok")
    return lax.ppermute(x, "tok", [(i, i ^ 1) for i in range(peers)])


def from_behind(x, by):
    peers = lax.axis_size("tok")
    return lax.ppermute(x, "tok", [(i, i + by) for i in range(peers - by)])


def sent_kernel(meta_ref, own, two, four, out_ref):
    tokens = own.shape[0]
    even = lax.rem(meta_ref[0], 2) == 0
    middle = two[...]
    out_ref[:tokens, :] = jnp.where(even, own[...], middle)
    out_ref[tokens:, :] = jnp.where(even, middle, four[...])


def swap_behind(meta, own, two, four):
    tokens, cols = own.shape
    arrays = [own, two, four]
    sent = kernel_call(
        sent_kernel,
        "sent_blocks",
        5,
        [SCALARS] + [HERE] * len(arrays),
        jax.ShapeDtypeStruct((2 * tokens, cols), own.dtype),
    )(meta, *arrays)
    return swap_cores(sent)


def chip_orders():
    peers = lax.axis_size("tok")
    bits = [1 << b for b in range(1, (peers - 1).bit_length())]
    turn = len(bits) // 2
    orders = (bits, bits[turn:] + bits[:turn])
    return [
        [(i, i ^ orders[i % 2][step]) for i in range(peers)] for step in range(len(bits))
    ]


def body(
    layer_input,
    input_norm_gain,
    query_weight,
    key_weight,
    value_weight,
    query_down_maps,
    value_down_maps,
    query_up_maps,
    value_up_maps,
    tenant_prompt_length,
    tenant_adapter_id,
    adapter_storage_slot,
):
    tok_rows = layer_input.shape[0]
    shares = lax.axis_size("mlp")
    lengths = tenant_prompt_length
    tenants = lengths.shape[0]
    places = jnp.stack([lax.axis_index("tok"), lax.axis_index("mlp"), jnp.int32(tenants)])
    meta = jnp.concatenate([places, lengths, tenant_adapter_id, adapter_storage_slot])
    first, first_sent, second, second_sent = pick(
        tenants, meta, query_down_maps, value_down_maps, query_up_maps, value_up_maps
    )
    orders = chip_orders()
    steps = len(orders)
    placed, first = lax.optimization_barrier((meta, first))
    indices = placed[:1] * tok_rows + jnp.arange(tok_rows, dtype=jnp.int32)
    cosine, sine = rotary_tables(positions_of(placed[HEADER : HEADER + tenants], indices))

    def shared(part):
        parts = [part]
        for bit in range(1, shares):
            parts.append(lax.ppermute(part, "mlp", [(i, i ^ bit) for i in range(shares)]))
        return parts

    sum_a = first + swap_cores(first_sent)
    got_a = lax.ppermute(sum_a, "tok", orders[0])
    gain, sum_a = lax.optimization_barrier((input_norm_gain[None, :], sum_a))
    normed, key, raw_value = project_kv(layer_input, gain, key_weight, value_weight, cosine, sine)
    sum_b = second + swap_cores(second_sent)
    got_a, key, sum_b = lax.optimization_barrier((got_a, key, sum_b))
    for step in range(1, steps):
        sum_a = sum_a + got_a
        got_a = lax.ppermute(sum_a, "tok", orders[step])
    normed, sum_a = lax.optimization_barrier((normed, sum_a))
    raw_query = project_query(normed, query_weight)
    got_a, raw_query = lax.optimization_barrier((got_a, raw_query))
    sum_a = sum_a + got_a
    other_a = swap_cores(sum_a)
    sum_b, key = lax.optimization_barrier((sum_b, key, sum_a))[:2]
    got_b = lax.ppermute(sum_b, "tok", orders[0])
    key_four, key_two = from_behind(key, 4), from_behind(key, 2)
    parts = shared(shrink(tenants, shares, meta, sum_a, other_a, normed))
    value = finish_value(tenants, meta, parts, sum_a, other_a, raw_value)
    value_four, value_two = from_behind(value, 4), from_behind(value, 2)
    for step in range(1, steps):
        sum_b = sum_b + got_b
        got_b = lax.ppermute(sum_b, "tok", orders[step])
    sum_b = sum_b + got_b
    other_b = swap_cores(sum_b)
    key_four, key_two = after(key_four, value), after(key_two, value)
    keys = [key_four, key_two, swap_behind(meta, key, key_two, key_four), key]
    query = finish_query(tenants, meta, parts, sum_b, other_b, raw_query, cosine, sine)
    early, totals = attention_weights(tenants, meta, query, keys)
    value_four, value_two, totals = lax.optimization_barrier((value_four, value_two, totals))
    values = [value_four, value_two, swap_behind(meta, value, value_two, value_four), value]
    return attend(tenants, meta, query, early, totals, keys, values)


def solution(mesh):
    placed = (
        P("tok", None),
        P(),
        P(None, "mlp"),
        P(None, "mlp"),
        P(None, "mlp"),
        P("tok", None, "mlp"),
        P("tok", None, "mlp"),
        P("tok", None, "mlp"),
        P("tok", None, "mlp"),
        P(),
        P(),
        P(),
    )
    return jax.shard_map(
        body, mesh=mesh, in_specs=placed, out_specs=P("tok", "mlp"), check_vma=False
    )
```

```python
import functools
import math

import jax
import jax.numpy as jnp
from jax import lax
from jax.experimental import pallas as pl
from jax.experimental.pallas import tpu as pltpu
from jax.sharding import PartitionSpec as P

HEAD_WIDTH = 128
ADAPTER_RANK = 16
LONGEST_PROMPT = 4
NORM_EPS = 1e-05
ROPE_BASE = 500000.0
ADAPTER_SCALE = 0.5
MIB = 1024 * 1024
TILE = 256
SLOT = 256
EARLY_TILES = 1


def rotary_tables(positions):
    half_width = HEAD_WIDTH // 2
    exponent = jnp.arange(half_width).astype(jnp.float32) * (2.0 / HEAD_WIDTH)
    inverse = jnp.exp(-exponent * jnp.log(jnp.float32(ROPE_BASE)))
    angles = positions[:, None] * inverse[None, :]
    cosine = jnp.cos(angles)
    sine = jnp.sin(angles)
    return jnp.concatenate([cosine, cosine], axis=1), jnp.concatenate([-sine, sine], axis=1)


def rope(x, cosine, sine):
    half = HEAD_WIDTH // 2
    swapped = jnp.concatenate([x[:, half:], x[:, :half]], axis=1)
    return x * cosine + swapped * sine


HERE = pl.BlockSpec(memory_space=pltpu.VMEM)
SCALARS = pl.BlockSpec(memory_space=pltpu.SMEM)
AWAY = pl.BlockSpec(memory_space=pltpu.HBM)


def kernel_call(kernel, name, mib, in_specs, out_shape, scratch_shapes=(), flops=0, bytes_accessed=0):
    return pl.pallas_call(
        kernel,
        in_specs=in_specs,
        out_specs=jax.tree.map(lambda _: HERE, out_shape),
        out_shape=out_shape,
        scratch_shapes=scratch_shapes,
        compiler_params=pltpu.CompilerParams(vmem_limit_bytes=mib * MIB),
        cost_estimate=pl.CostEstimate(
            flops=flops, bytes_accessed=bytes_accessed, transcendentals=0
        ),
        name=name,
    )


HEADER = 3


def tenant_at(meta_ref, tenants, index):
    tid = jnp.zeros(index.shape, jnp.int32)
    start = jnp.zeros(index.shape, jnp.int32)
    end = 0
    for t in range(tenants):
        end = end + meta_ref[HEADER + t]
        past = index >= end
        tid = jnp.where(past, t + 1, tid)
        start = jnp.where(past, end, start)
    return tid, start


def pick_kernel(tenants, meta_ref, qd, vd, qu, vu, *refs):
    *outs, position_ref, sems = refs
    device = meta_ref[0]
    core = lax.rem(device, 2)
    rank = ADAPTER_RANK
    held, _, wide = qd.shape
    narrow = vu.shape[2] // 2
    count = tenants // 2
    ids = HEADER + tenants
    slots = ids + tenants
    jobs = []
    for side in range(2):
        half = core if side == 0 else 1 - core
        for t in range(count):
            slot = meta_ref[slots + meta_ref[ids + half * count + t]] - device * held
            here = (slot >= 0) & (slot < held)
            jobs.append((side, t, jnp.clip(slot, 0, held - 1), here))

    def copies(side, t, slot):
        first, second = outs[side], outs[2 + side]
        top = pl.ds(2 * t * rank, rank)
        low = pl.ds((2 * t + 1) * rank, rank)
        pairs = (
            (qd.at[slot], first.at[top, pl.ds(0, wide)]),
            (vd.at[slot], first.at[low, pl.ds(0, wide)]),
            (vu.at[slot, :, pl.ds(0, narrow)], first.at[top, pl.ds(wide, narrow)]),
            (vu.at[slot, :, pl.ds(narrow, narrow)], first.at[low, pl.ds(wide, narrow)]),
            (qu.at[slot], second.at[pl.ds(t * rank, rank), :]),
        )
        return [
            pltpu.make_async_copy(source, target, sems.at[side * count + t, number])
            for number, (source, target) in enumerate(pairs)
        ]

    for side, t, slot, here in jobs:

        @pl.when(here)
        def _(side=side, t=t, slot=slot):
            for copy in copies(side, t, slot):
                copy.start()

    for side, t, slot, here in jobs:
        first, second = outs[side], outs[2 + side]

        @pl.when(jnp.logical_not(here))
        def _(first=first, second=second, t=t):
            first[2 * t * rank : 2 * (t + 1) * rank, :] = jnp.zeros(
                (2 * rank, wide + narrow), jnp.bfloat16
            )
            second[t * rank : (t + 1) * rank, :] = jnp.zeros((rank, wide), jnp.bfloat16)

    tokens = position_ref.shape[1]
    index = device * tokens + lax.broadcasted_iota(jnp.int32, (1, tokens), 1)
    _, start = tenant_at(meta_ref, tenants, index)
    position_ref[...] = (index - start).astype(jnp.float32)

    for side, t, slot, here in jobs:

        @pl.when(here)
        def _(side=side, t=t, slot=slot):
            for copy in copies(side, t, slot):
                copy.wait()


def pick(tenants, tokens, meta, qd, vd, qu, vu):
    held, rank, wide = qd.shape
    narrow = vu.shape[2] // 2
    rows = tenants * rank
    shapes = ((rows, wide + narrow),) * 2 + ((rows // 2, wide),) * 2
    maps = [pltpu.with_memory_space_constraint(x, pltpu.HBM) for x in (qd, vd, qu, vu)]
    return kernel_call(
        functools.partial(pick_kernel, tenants),
        "pick_adapters",
        4,
        [SCALARS] + [AWAY] * 4,
        [jax.ShapeDtypeStruct(shape, jnp.bfloat16) for shape in shapes]
        + [jax.ShapeDtypeStruct((1, tokens), jnp.float32)],
        [pltpu.SemaphoreType.DMA((tenants, 5))],
    )(meta, *maps)


def kv_kernel(gain_ref, cos_ref, sin_ref, x, wk, wv, normed, key_ref, value_ref):
    rows = x.shape[0]
    width = HEAD_WIDTH
    step = rows // 4
    for top in range(0, rows, step):
        at = slice(top, top + step)
        wide = x[at, :].astype(jnp.float32)
        scale = lax.rsqrt(jnp.mean(wide * wide, axis=1, keepdims=True) + NORM_EPS)
        normed[at, :] = (wide * scale * gain_ref[...]).astype(jnp.bfloat16)
    raw = jnp.dot(normed[...], wk[...], preferred_element_type=jnp.float32)
    for head in range(key_ref.shape[1] // width):
        cols = slice(head * width, (head + 1) * width)
        key_ref[:, cols] = rope(raw[:, cols], cos_ref[...], sin_ref[...]).astype(jnp.bfloat16)
    value_ref[...] = jnp.dot(normed[...], wv[...], preferred_element_type=jnp.float32)


def project_kv(x, gain, wk, wv, cosine, sine):
    rows, model = x.shape
    cols = wk.shape[1]
    return kernel_call(
        kv_kernel,
        "norm_key_value",
        16,
        [HERE] * 6,
        [
            jax.ShapeDtypeStruct((rows, model), jnp.bfloat16),
            jax.ShapeDtypeStruct((rows, cols), jnp.bfloat16),
            jax.ShapeDtypeStruct((rows, cols), jnp.float32),
        ],
        flops=4 * rows * model * cols,
        bytes_accessed=4 * model * (rows + cols),
    )(gain, cosine, sine, x, wk, wv)


def query_projection_kernel(x, w, out_ref):
    tile = 256
    for at in range(0, w.shape[1], tile):
        out_ref[:, at : at + tile] = jnp.dot(
            x[...], w[:, at : at + tile], preferred_element_type=jnp.float32
        )


def project_query(normed, weight):
    rows, model = normed.shape
    cols = weight.shape[1]
    return kernel_call(
        query_projection_kernel,
        "query_projection",
        16,
        [HERE, HERE],
        jax.ShapeDtypeStruct((rows, cols), jnp.float32),
        flops=2 * rows * model * cols,
        bytes_accessed=2 * model * (rows + cols),
    )(normed, weight)


def shrink_kernel(tenants, shares, meta_ref, own_ref, other_ref, x, out_ref):
    contract = (((1,), (1,)), ((), ()))
    tokens, model = x.shape
    kept = model // shares
    part = x[:, pl.ds(pl.multiple_of(meta_ref[1] * kept, kept), kept)]
    rows = 2 * ADAPTER_RANK
    count = tenants // 2
    core = lax.rem(meta_ref[0], 2)
    index = meta_ref[0] * tokens + lax.broadcasted_iota(jnp.int32, (1, tokens), 1)
    tid, _ = tenant_at(meta_ref, tenants, index)
    total = jnp.zeros((rows, tokens), jnp.float32)
    for ref, half in ((own_ref, core), (other_ref, 1 - core)):
        wide = lax.dot_general(ref[:, :kept], part, contract, preferred_element_type=jnp.float32)
        for t in range(count):
            total = total + jnp.where(
                tid == half * count + t, wide[t * rows : (t + 1) * rows, :], 0.0
            )
    out_ref[...] = total


def shrink(tenants, shares, meta, own, other, normed):
    return kernel_call(
        functools.partial(shrink_kernel, tenants, shares),
        "shrink_share",
        8,
        [SCALARS, HERE, HERE, HERE],
        jax.ShapeDtypeStruct((2 * ADAPTER_RANK, normed.shape[0]), jnp.float32),
    )(meta, own, other, normed)


def spread_tenants(tenants, parts, rows, meta_ref):
    parts = [part[rows, :] for part in parts]
    while len(parts) > 1:
        parts = [parts[i] + parts[i + 1] for i in range(0, len(parts), 2)]
    shrunk = parts[0]
    rank, tokens = shrunk.shape
    lanes = tenants * rank
    lane = lax.broadcasted_iota(jnp.int32, (rank, lanes), 1)
    repeat = (lane % rank == lax.broadcasted_iota(jnp.int32, (rank, lanes), 0)).astype(
        jnp.bfloat16
    )
    wide = lax.dot_general(
        shrunk.astype(jnp.bfloat16),
        repeat,
        (((0,), (0,)), ((), ())),
        preferred_element_type=jnp.float32,
    )
    index = meta_ref[0] * tokens + lax.broadcasted_iota(jnp.int32, (tokens, 1), 0)
    tid, _ = tenant_at(meta_ref, tenants, index)
    owner = lax.broadcasted_iota(jnp.int32, (1, lanes), 1) // rank
    return jnp.where(owner == tid, wide, 0.0).astype(jnp.bfloat16)


def value_kernel(tenants, shares, meta_ref, *refs):
    parts = refs[:shares]
    own_ref, other_ref, raw_ref, out_ref = refs[shares:]
    side = own_ref.shape[1] - raw_ref.shape[1] // 2
    rank = ADAPTER_RANK
    spread = spread_tenants(tenants, parts, slice(rank, 2 * rank), meta_ref)
    even = lax.rem(meta_ref[0], 2) == 0
    own, other = (
        jnp.concatenate(
            [
                jnp.concatenate(
                    [ref[top : top + rank, side:], ref[top + rank : top + 2 * rank, side:]], axis=1
                )
                for top in range(0, ref.shape[0], 2 * rank)
            ],
            axis=0,
        )
        for ref in (own_ref, other_ref)
    )
    up = jnp.concatenate([jnp.where(even, own, other), jnp.where(even, other, own)], axis=0)
    delta = jnp.dot(spread, up, preferred_element_type=jnp.float32)
    out_ref[...] = (raw_ref[...] + ADAPTER_SCALE * delta).astype(jnp.bfloat16)


def finish_value(tenants, meta, parts, own, other, raw):
    return kernel_call(
        functools.partial(value_kernel, tenants, len(parts)),
        "value_rows",
        5,
        [SCALARS] + [HERE] * (len(parts) + 3),
        jax.ShapeDtypeStruct(raw.shape, jnp.bfloat16),
    )(meta, *parts, own, other, raw)


def query_kernel(tenants, shares, meta_ref, *refs):
    rank = ADAPTER_RANK
    parts = refs[:shares]
    own_ref, other_ref, raw_ref, cos_ref, sin_ref, out_ref = refs[shares:]
    spread = spread_tenants(tenants, parts, slice(0, rank), meta_ref)
    even = lax.rem(meta_ref[0], 2) == 0
    own, other = own_ref[...], other_ref[...]
    up = jnp.concatenate([jnp.where(even, own, other), jnp.where(even, other, own)], axis=0)
    for top in range(0, raw_ref.shape[1], 2 * HEAD_WIDTH):
        delta = jnp.dot(
            spread, up[:, top : top + 2 * HEAD_WIDTH], preferred_element_type=jnp.float32
        )
        for head in range(2):
            local = slice(head * HEAD_WIDTH, (head + 1) * HEAD_WIDTH)
            cols = slice(top + head * HEAD_WIDTH, top + (head + 1) * HEAD_WIDTH)
            row = raw_ref[:, cols] + ADAPTER_SCALE * delta[:, local]
            out_ref[:, cols] = rope(row, cos_ref[...], sin_ref[...]).astype(jnp.bfloat16)


def finish_query(tenants, meta, parts, own, other, raw, cosine, sine):
    return kernel_call(
        functools.partial(query_kernel, tenants, len(parts)),
        "query_rows",
        8,
        [SCALARS] + [HERE] * (len(parts) + 5),
        jax.ShapeDtypeStruct(raw.shape, jnp.bfloat16),
    )(meta, *parts, own, other, raw, cosine, sine)


def tile_bounds(tenants, meta_ref, tokens):
    base = (meta_ref[0] - LONGEST_PROMPT) * tokens
    behind = LONGEST_PROMPT * tokens

    def start_of(index):
        start = 0
        end = 0
        for t in range(tenants):
            end = end + meta_ref[HEADER + t]
            start = jnp.where(index >= end, end, start)
        return start - base

    bounds = []
    for begin in range(behind, behind + tokens, TILE):
        low = start_of(base + begin)
        high = start_of(base + begin + TILE - 1)
        bounds.append((jnp.minimum(low // SLOT, behind // SLOT), high))
    return bounds


def line_up(target, four, two, odd, own):
    tokens = own.shape[0]
    target[:tokens, :] = four[...]
    target[tokens : 2 * tokens, :] = odd[tokens:, :]
    target[2 * tokens : 3 * tokens, :] = two[...]
    target[3 * tokens : 4 * tokens, :] = odd[:tokens, :]
    target[4 * tokens :, :] = own[...]


def head_rows(all_heads, groups):
    width = HEAD_WIDTH
    found = []
    for head in range(all_heads):
        group = head * groups // all_heads
        found.append(
            (
                slice(head * TILE, (head + 1) * TILE),
                slice(head * width, (head + 1) * width),
                slice(group * width, (group + 1) * width),
            )
        )
    return found


def weights_kernel(
    tenants, meta_ref, q_ref, k4, k2, k31, k0, probs, totals, keys, scores, bias, peaks
):
    width = HEAD_WIDTH
    tokens = q_ref.shape[0]
    behind = LONGEST_PROMPT * tokens
    slots = behind // SLOT
    factor = HEAD_WIDTH ** (-0.5) * math.log2(math.e)
    base = (meta_ref[0] - LONGEST_PROMPT) * tokens
    line_up(keys, k4, k2, k31, k0)
    mine = behind + lax.broadcasted_iota(jnp.int32, (tokens, 1), 0)
    _, start = tenant_at(meta_ref, tenants, base + mine)
    start = start - base
    subs = head_rows(q_ref.shape[1] // width, k0.shape[1] // width)
    bounds = tile_bounds(tenants, meta_ref, tokens)

    for tile, (first, high) in enumerate(bounds[:EARLY_TILES]):
        top = slice(tile * TILE, (tile + 1) * TILE)
        odd = lax.rem(first, 2) == 1
        own_slots = (tile + 1) * TILE // SLOT

        def score(slot, count, masked, fresh=False, top=top):
            at_keys = pl.ds(pl.multiple_of(slot * SLOT, SLOT), count * SLOT)
            if masked:
                place = slot * SLOT + lax.broadcasted_iota(jnp.int32, (TILE, count * SLOT), 1)
                seen = (place >= start[top]) & (place <= mine[top])
                bias[:, : count * SLOT] = jnp.where(seen, 0.0, -jnp.inf)
            for at, head, group in subs:
                raw = lax.dot_general(
                    q_ref[top, head],
                    keys[at_keys, group],
                    (((1,), (1,)), ((), ())),
                    preferred_element_type=jnp.float32,
                )
                best = None if fresh else peaks[at, :]
                for piece in range(count * SLOT // width):
                    cols = slice(piece * width, (piece + 1) * width)
                    part = raw[:, cols] * factor
                    if masked:
                        part = part + bias[:, cols]
                    inner = piece * width % SLOT
                    scores[slot + piece * width // SLOT, at, inner : inner + width] = part
                    best = part if best is None else jnp.maximum(best, part)
                peaks[at, :] = best

        def weigh(slot, count, fresh=False, tile=tile):
            for at, _, _ in subs:
                peak = peaks[at, :]
                total = None if fresh else totals[tile, at, :]
                for piece in range(count * SLOT // width):
                    inner = piece * width % SLOT
                    place = slot + piece * width // SLOT
                    weights = jnp.exp2(scores[place, at, inner : inner + width] - peak)
                    total = weights if total is None else total + weights
                    probs[tile, place, at, inner : inner + width] = weights.astype(jnp.bfloat16)
                totals[tile, at, :] = total

        def pair(c, carry, high=high, score=score):
            edge = c * 2 * SLOT < high
            pl.when(edge)(lambda: score(2 * c, 2, True))
            pl.when(jnp.logical_not(edge))(lambda: score(2 * c, 2, False))
            return carry

        def weigh_pair(c, carry, weigh=weigh):
            weigh(2 * c, 2)
            return carry

        score(slots, own_slots, True, fresh=True)
        pl.when(odd)(lambda: score(first, 1, True))
        lax.fori_loop((first + 1) // 2, slots // 2, pair, 0)
        for at, _, _ in subs:
            peaks[at, :] = jnp.broadcast_to(
                jnp.max(peaks[at, :], axis=1, keepdims=True), (TILE, width)
            )
        weigh(slots, own_slots, fresh=True)
        pl.when(odd)(lambda: weigh(first, 1))
        lax.fori_loop((first + 1) // 2, slots // 2, weigh_pair, 0)


def attention_weights(tenants, meta, query, keys):
    tokens, cols = query.shape
    kv_cols = keys[-1].shape[1]
    rows = cols // HEAD_WIDTH * TILE
    span = (LONGEST_PROMPT + 1) * tokens
    slots = span // SLOT
    tiles = EARLY_TILES
    return pl.pallas_call(
        functools.partial(weights_kernel, tenants),
        in_specs=[SCALARS] + [HERE] * (1 + len(keys)),
        out_specs=[HERE, HERE],
        out_shape=[
            pltpu.VMEM((tiles, slots, rows, SLOT), jnp.bfloat16),
            pltpu.VMEM((tiles, rows, HEAD_WIDTH), jnp.float32),
        ],
        scratch_shapes=[
            pltpu.VMEM((span, kv_cols), jnp.bfloat16),
            pltpu.VMEM((slots, rows, SLOT), jnp.float32),
            pltpu.VMEM((TILE, 2 * SLOT), jnp.float32),
            pltpu.VMEM((rows, HEAD_WIDTH), jnp.float32),
        ],
        compiler_params=pltpu.CompilerParams(vmem_limit_bytes=30 * MIB),
        cost_estimate=pl.CostEstimate(flops=0, bytes_accessed=0, transcendentals=0),
        name="attention_weights",
    )(meta, query, *keys)


def attend_kernel(
    tenants, meta_ref, q_ref, early, early_totals, k4, k2, k31, k0, v4, v2, v31, v0, out_ref,
    keys, values, scores, bias, peaks, totals, mixed,
):
    width = HEAD_WIDTH
    tokens = q_ref.shape[0]
    behind = LONGEST_PROMPT * tokens
    slots = behind // SLOT
    factor = HEAD_WIDTH ** (-0.5) * math.log2(math.e)
    base = (meta_ref[0] - LONGEST_PROMPT) * tokens
    line_up(keys, k4, k2, k31, k0)
    line_up(values, v4, v2, v31, v0)
    mine = behind + lax.broadcasted_iota(jnp.int32, (tokens, 1), 0)
    _, start = tenant_at(meta_ref, tenants, base + mine)
    start = start - base
    subs = head_rows(q_ref.shape[1] // width, k0.shape[1] // width)
    bounds = tile_bounds(tenants, meta_ref, tokens)

    for tile, (first, _) in enumerate(bounds[:EARLY_TILES]):
        top = slice(tile * TILE, (tile + 1) * TILE)

        def mix_early(slot, count, fresh=False, tile=tile):
            at_values = pl.ds(pl.multiple_of(slot * SLOT, SLOT), count * SLOT)
            for at, _, group in subs:
                part = jnp.dot(
                    jnp.concatenate(
                        [early[tile, slot + step, at, :] for step in range(count)], axis=1
                    ),
                    values[at_values, group],
                    preferred_element_type=jnp.float32,
                )
                if fresh:
                    mixed[at, :] = part
                else:
                    mixed[at, :] += part

        def early_pair(c, carry, mix_early=mix_early):
            mix_early(2 * c, 2)
            return carry

        mix_early(slots, (tile + 1) * TILE // SLOT, fresh=True)
        pl.when(lax.rem(first, 2) == 1)(lambda: mix_early(first, 1))
        lax.fori_loop((first + 1) // 2, slots // 2, early_pair, 0)
        for at, head, _ in subs:
            total = jnp.sum(early_totals[tile, at, :], axis=1, keepdims=True)
            out_ref[top, head] = (mixed[at, :] / total).astype(jnp.bfloat16)

    for tile in range(EARLY_TILES, tokens // TILE):
        top = slice(tile * TILE, (tile + 1) * TILE)
        first, high = bounds[tile]
        odd = lax.rem(first, 2) == 1
        own_slots = (tile + 1) * TILE // SLOT

        def columns(slot, count):
            return pl.ds(pl.multiple_of(slot * SLOT, SLOT), count * SLOT)

        def score(slot, count, masked, fresh=False, top=top):
            at_keys = columns(slot, count)
            if masked:
                place = slot * SLOT + lax.broadcasted_iota(jnp.int32, (TILE, count * SLOT), 1)
                seen = (place >= start[top]) & (place <= mine[top])
                bias[:, : count * SLOT] = jnp.where(seen, 0.0, -jnp.inf)
            for at, head, group in subs:
                raw = lax.dot_general(
                    q_ref[top, head],
                    keys[at_keys, group],
                    (((1,), (1,)), ((), ())),
                    preferred_element_type=jnp.float32,
                )
                best = None if fresh else peaks[at, :]
                for piece in range(count * SLOT // width):
                    cols = slice(piece * width, (piece + 1) * width)
                    part = raw[:, cols] * factor
                    if masked:
                        part = part + bias[:, cols]
                    inner = piece * width % SLOT
                    scores[slot + piece * width // SLOT, at, inner : inner + width] = part
                    best = part if best is None else jnp.maximum(best, part)
                peaks[at, :] = best

        def mix(slot, count, fresh=False):
            at_values = columns(slot, count)
            for at, _, group in subs:
                peak = peaks[at, :]
                total = None if fresh else totals[at, :]
                probs = []
                for piece in range(count * SLOT // width):
                    inner = piece * width % SLOT
                    weights = jnp.exp2(
                        scores[slot + piece * width // SLOT, at, inner : inner + width] - peak
                    )
                    total = weights if total is None else total + weights
                    probs.append(weights.astype(jnp.bfloat16))
                totals[at, :] = total
                part = jnp.dot(
                    jnp.concatenate(probs, axis=1),
                    values[at_values, group],
                    preferred_element_type=jnp.float32,
                )
                if fresh:
                    mixed[at, :] = part
                else:
                    mixed[at, :] += part

        def pair(c, carry, high=high, score=score):
            edge = c * 2 * SLOT < high
            pl.when(edge)(lambda: score(2 * c, 2, True))
            pl.when(jnp.logical_not(edge))(lambda: score(2 * c, 2, False))
            return carry

        def mix_pair(c, carry, mix=mix):
            mix(2 * c, 2)
            return carry

        score(slots, own_slots, True, fresh=True)
        pl.when(odd)(lambda: score(first, 1, True))
        lax.fori_loop((first + 1) // 2, slots // 2, pair, 0)
        for at, _, _ in subs:
            peaks[at, :] = jnp.broadcast_to(
                jnp.max(peaks[at, :], axis=1, keepdims=True), (TILE, width)
            )
        mix(slots, own_slots, fresh=True)
        pl.when(odd)(lambda: mix(first, 1))
        lax.fori_loop((first + 1) // 2, slots // 2, mix_pair, 0)
        for at, head, _ in subs:
            total = jnp.sum(totals[at, :], axis=1, keepdims=True)
            out_ref[top, head] = (mixed[at, :] / total).astype(jnp.bfloat16)


def attend(tenants, meta, query, early, early_totals, keys, values):
    tokens, cols = query.shape
    kv_cols = keys[-1].shape[1]
    rows = cols // HEAD_WIDTH * TILE
    span = (LONGEST_PROMPT + 1) * tokens
    return kernel_call(
        functools.partial(attend_kernel, tenants),
        "attention",
        36,
        [SCALARS] + [HERE] * (3 + len(keys) + len(values)),
        jax.ShapeDtypeStruct((tokens, cols), jnp.bfloat16),
        [
            pltpu.VMEM((span, kv_cols), jnp.bfloat16),
            pltpu.VMEM((span, kv_cols), jnp.bfloat16),
            pltpu.VMEM((span // SLOT, rows, SLOT), jnp.float32),
            pltpu.VMEM((TILE, 2 * SLOT), jnp.float32),
            pltpu.VMEM((rows, HEAD_WIDTH), jnp.float32),
            pltpu.VMEM((rows, HEAD_WIDTH), jnp.float32),
            pltpu.VMEM((rows, HEAD_WIDTH), jnp.float32),
        ],
    )(meta, query, early, early_totals, *keys, *values)


def after(value, *others):
    return lax.optimization_barrier((value,) + others)[0]


def swap_cores(x):
    peers = lax.axis_size("tok")
    return lax.ppermute(x, "tok", [(i, i ^ 1) for i in range(peers)])


def from_behind(x, by):
    peers = lax.axis_size("tok")
    return lax.ppermute(x, "tok", [(i, i + by) for i in range(peers - by)])


def sent_kernel(meta_ref, own, two, four, out_ref):
    tokens = own.shape[0]
    even = lax.rem(meta_ref[0], 2) == 0
    middle = two[...]
    out_ref[:tokens, :] = jnp.where(even, own[...], middle)
    out_ref[tokens:, :] = jnp.where(even, middle, four[...])


def swap_behind(meta, own, two, four):
    tokens, cols = own.shape
    arrays = [own, two, four]
    sent = kernel_call(
        sent_kernel,
        "sent_blocks",
        5,
        [SCALARS] + [HERE] * len(arrays),
        jax.ShapeDtypeStruct((2 * tokens, cols), own.dtype),
    )(meta, *arrays)
    return swap_cores(sent)


def chip_orders():
    peers = lax.axis_size("tok")
    bits = [1 << b for b in range(1, (peers - 1).bit_length())]
    turn = len(bits) // 2
    orders = (bits, bits[turn:] + bits[:turn])
    return [
        [(i, i ^ orders[i % 2][step]) for i in range(peers)] for step in range(len(bits))
    ]


def body(
    layer_input,
    input_norm_gain,
    query_weight,
    key_weight,
    value_weight,
    query_down_maps,
    value_down_maps,
    query_up_maps,
    value_up_maps,
    tenant_prompt_length,
    tenant_adapter_id,
    adapter_storage_slot,
):
    tok_rows = layer_input.shape[0]
    shares = lax.axis_size("mlp")
    lengths = tenant_prompt_length
    tenants = lengths.shape[0]
    places = jnp.stack([lax.axis_index("tok"), lax.axis_index("mlp"), jnp.int32(tenants)])
    meta = jnp.concatenate([places, lengths, tenant_adapter_id, adapter_storage_slot])
    first, first_sent, second, second_sent, positions = pick(
        tenants, tok_rows, meta, query_down_maps, value_down_maps, query_up_maps, value_up_maps
    )
    orders = chip_orders()
    steps = len(orders)
    cosine, sine = rotary_tables(positions[0])

    def shared(part):
        parts = [part]
        for bit in range(1, shares):
            parts.append(lax.ppermute(part, "mlp", [(i, i ^ bit) for i in range(shares)]))
        return parts

    sum_a = first + swap_cores(first_sent)
    got_a = lax.ppermute(sum_a, "tok", orders[0])
    gain, sum_a = lax.optimization_barrier((input_norm_gain[None, :], sum_a))
    normed, key, raw_value = project_kv(layer_input, gain, key_weight, value_weight, cosine, sine)
    sum_b = second + swap_cores(second_sent)
    got_a, key, sum_b = lax.optimization_barrier((got_a, key, sum_b))
    for step in range(1, steps):
        sum_a = sum_a + got_a
        got_a = lax.ppermute(sum_a, "tok", orders[step])
    normed, sum_a = lax.optimization_barrier((normed, sum_a))
    raw_query = project_query(normed, query_weight)
    got_a, raw_query = lax.optimization_barrier((got_a, raw_query))
    sum_a = sum_a + got_a
    other_a = swap_cores(sum_a)
    sum_b, key = lax.optimization_barrier((sum_b, key, sum_a))[:2]
    got_b = lax.ppermute(sum_b, "tok", orders[0])
    key_four, key_two = from_behind(key, 4), from_behind(key, 2)
    parts = shared(shrink(tenants, shares, meta, sum_a, other_a, normed))
    value = finish_value(tenants, meta, parts, sum_a, other_a, raw_value)
    value_four, value_two = from_behind(value, 4), from_behind(value, 2)
    for step in range(1, steps):
        sum_b = sum_b + got_b
        got_b = lax.ppermute(sum_b, "tok", orders[step])
    sum_b = sum_b + got_b
    other_b = swap_cores(sum_b)
    key_four, key_two = after(key_four, value), after(key_two, value)
    keys = [key_four, key_two, swap_behind(meta, key, key_two, key_four), key]
    query = finish_query(tenants, meta, parts, sum_b, other_b, raw_query, cosine, sine)
    early, totals = attention_weights(tenants, meta, query, keys)
    value_four, value_two, totals = lax.optimization_barrier((value_four, value_two, totals))
    values = [value_four, value_two, swap_behind(meta, value, value_two, value_four), value]
    return attend(tenants, meta, query, early, totals, keys, values)


def solution(mesh):
    placed = (
        P("tok", None),
        P(),
        P(None, "mlp"),
        P(None, "mlp"),
        P(None, "mlp"),
        P("tok", None, "mlp"),
        P("tok", None, "mlp"),
        P("tok", None, "mlp"),
        P("tok", None, "mlp"),
        P(),
        P(),
        P(),
    )
    return jax.shard_map(
        body, mesh=mesh, in_specs=placed, out_specs=P("tok", "mlp"), check_vma=False
    )
```

```python
import functools
import math

import jax
import jax.numpy as jnp
from jax import lax
from jax.experimental import pallas as pl
from jax.experimental.pallas import tpu as pltpu
from jax.sharding import PartitionSpec as P

HEAD_WIDTH = 128
ADAPTER_RANK = 16
LONGEST_PROMPT = 4
NORM_EPS = 1e-05
ROPE_BASE = 500000.0
ADAPTER_SCALE = 0.5
MIB = 1024 * 1024
TILE = 256
SLOT = 256
EARLY_TILES = 1


def rotary_tables(positions):
    half_width = HEAD_WIDTH // 2
    exponent = jnp.arange(half_width).astype(jnp.float32) * (2.0 / HEAD_WIDTH)
    inverse = jnp.exp(-exponent * jnp.log(jnp.float32(ROPE_BASE)))
    angles = positions[:, None] * inverse[None, :]
    cosine = jnp.cos(angles)
    sine = jnp.sin(angles)
    return jnp.concatenate([cosine, cosine], axis=1), jnp.concatenate([-sine, sine], axis=1)


def rope(x, cosine, sine):
    half = HEAD_WIDTH // 2
    swapped = jnp.concatenate([x[:, half:], x[:, :half]], axis=1)
    return x * cosine + swapped * sine


HERE = pl.BlockSpec(memory_space=pltpu.VMEM)
SCALARS = pl.BlockSpec(memory_space=pltpu.SMEM)
AWAY = pl.BlockSpec(memory_space=pltpu.HBM)


def kernel_call(kernel, name, mib, in_specs, out_shape, scratch_shapes=(), flops=0, bytes_accessed=0):
    return pl.pallas_call(
        kernel,
        in_specs=in_specs,
        out_specs=jax.tree.map(lambda _: HERE, out_shape),
        out_shape=out_shape,
        scratch_shapes=scratch_shapes,
        compiler_params=pltpu.CompilerParams(vmem_limit_bytes=mib * MIB),
        cost_estimate=pl.CostEstimate(
            flops=flops, bytes_accessed=bytes_accessed, transcendentals=0
        ),
        name=name,
    )


HEADER = 3


def tenant_at(meta_ref, tenants, index):
    tid = jnp.zeros(index.shape, jnp.int32)
    start = jnp.zeros(index.shape, jnp.int32)
    end = 0
    for t in range(tenants):
        end = end + meta_ref[HEADER + t]
        past = index >= end
        tid = jnp.where(past, t + 1, tid)
        start = jnp.where(past, end, start)
    return tid, start


def pick_kernel(tenants, meta_ref, qd, vd, qu, vu, *refs):
    *outs, position_ref, sems = refs
    device = meta_ref[0]
    core = lax.rem(device, 2)
    rank = ADAPTER_RANK
    held, _, wide = qd.shape
    narrow = vu.shape[2] // 2
    count = tenants // 2
    ids = HEADER + tenants
    slots = ids + tenants
    jobs = []
    for side in range(2):
        half = core if side == 0 else 1 - core
        for t in range(count):
            slot = meta_ref[slots + meta_ref[ids + half * count + t]] - device * held
            here = (slot >= 0) & (slot < held)
            jobs.append((side, t, jnp.clip(slot, 0, held - 1), here))

    def copies(side, t, slot):
        first, second = outs[side], outs[2 + side]
        top = pl.ds(2 * t * rank, rank)
        low = pl.ds((2 * t + 1) * rank, rank)
        pairs = (
            (qd.at[slot], first.at[top, pl.ds(0, wide)]),
            (vd.at[slot], first.at[low, pl.ds(0, wide)]),
            (vu.at[slot, :, pl.ds(0, narrow)], first.at[top, pl.ds(wide, narrow)]),
            (vu.at[slot, :, pl.ds(narrow, narrow)], first.at[low, pl.ds(wide, narrow)]),
            (qu.at[slot], second.at[pl.ds(t * rank, rank), :]),
        )
        return [
            pltpu.make_async_copy(source, target, sems.at[side * count + t, number])
            for number, (source, target) in enumerate(pairs)
        ]

    for side, t, slot, here in jobs:

        @pl.when(here)
        def _(side=side, t=t, slot=slot):
            for copy in copies(side, t, slot):
                copy.start()

    for side, t, slot, here in jobs:
        first, second = outs[side], outs[2 + side]

        @pl.when(jnp.logical_not(here))
        def _(first=first, second=second, t=t):
            first[2 * t * rank : 2 * (t + 1) * rank, :] = jnp.zeros(
                (2 * rank, wide + narrow), jnp.bfloat16
            )
            second[t * rank : (t + 1) * rank, :] = jnp.zeros((rank, wide), jnp.bfloat16)

    tokens = position_ref.shape[1]
    index = device * tokens + lax.broadcasted_iota(jnp.int32, (1, tokens), 1)
    _, start = tenant_at(meta_ref, tenants, index)
    position_ref[...] = (index - start).astype(jnp.float32)

    for side, t, slot, here in jobs:

        @pl.when(here)
        def _(side=side, t=t, slot=slot):
            for copy in copies(side, t, slot):
                copy.wait()


def pick(tenants, tokens, meta, qd, vd, qu, vu):
    held, rank, wide = qd.shape
    narrow = vu.shape[2] // 2
    rows = tenants * rank
    shapes = ((rows, wide + narrow),) * 2 + ((rows // 2, wide),) * 2
    maps = [pltpu.with_memory_space_constraint(x, pltpu.HBM) for x in (qd, vd, qu, vu)]
    return kernel_call(
        functools.partial(pick_kernel, tenants),
        "pick_adapters",
        4,
        [SCALARS] + [AWAY] * 4,
        [jax.ShapeDtypeStruct(shape, jnp.bfloat16) for shape in shapes]
        + [jax.ShapeDtypeStruct((1, tokens), jnp.float32)],
        [pltpu.SemaphoreType.DMA((tenants, 5))],
    )(meta, *maps)


def kv_kernel(gain_ref, cos_ref, sin_ref, x, wk, wv, normed, key_ref, value_ref):
    rows = x.shape[0]
    width = HEAD_WIDTH
    step = rows // 4
    for top in range(0, rows, step):
        at = slice(top, top + step)
        wide = x[at, :].astype(jnp.float32)
        scale = lax.rsqrt(jnp.mean(wide * wide, axis=1, keepdims=True) + NORM_EPS)
        normed[at, :] = (wide * scale * gain_ref[...]).astype(jnp.bfloat16)
    raw = jnp.dot(normed[...], wk[...], preferred_element_type=jnp.float32)
    for head in range(key_ref.shape[1] // width):
        cols = slice(head * width, (head + 1) * width)
        key_ref[:, cols] = rope(raw[:, cols], cos_ref[...], sin_ref[...]).astype(jnp.bfloat16)
    value_ref[...] = jnp.dot(normed[...], wv[...], preferred_element_type=jnp.float32)


def project_kv(x, gain, wk, wv, cosine, sine):
    rows, model = x.shape
    cols = wk.shape[1]
    return kernel_call(
        kv_kernel,
        "norm_key_value",
        16,
        [HERE] * 6,
        [
            jax.ShapeDtypeStruct((rows, model), jnp.bfloat16),
            jax.ShapeDtypeStruct((rows, cols), jnp.bfloat16),
            jax.ShapeDtypeStruct((rows, cols), jnp.float32),
        ],
        flops=4 * rows * model * cols,
        bytes_accessed=4 * model * (rows + cols),
    )(gain, cosine, sine, x, wk, wv)


def query_projection_kernel(x, w, out_ref):
    tile = 256
    for at in range(0, w.shape[1], tile):
        out_ref[:, at : at + tile] = jnp.dot(
            x[...], w[:, at : at + tile], preferred_element_type=jnp.float32
        )


def project_query(normed, weight):
    rows, model = normed.shape
    cols = weight.shape[1]
    return kernel_call(
        query_projection_kernel,
        "query_projection",
        16,
        [HERE, HERE],
        jax.ShapeDtypeStruct((rows, cols), jnp.float32),
        flops=2 * rows * model * cols,
        bytes_accessed=2 * model * (rows + cols),
    )(normed, weight)


def shrink_kernel(tenants, shares, meta_ref, own_ref, other_ref, x, out_ref):
    contract = (((1,), (1,)), ((), ()))
    tokens, model = x.shape
    kept = model // shares
    part = x[:, pl.ds(pl.multiple_of(meta_ref[1] * kept, kept), kept)]
    rows = 2 * ADAPTER_RANK
    count = tenants // 2
    core = lax.rem(meta_ref[0], 2)
    index = meta_ref[0] * tokens + lax.broadcasted_iota(jnp.int32, (1, tokens), 1)
    tid, _ = tenant_at(meta_ref, tenants, index)
    total = jnp.zeros((rows, tokens), jnp.float32)
    for ref, half in ((own_ref, core), (other_ref, 1 - core)):
        wide = lax.dot_general(ref[:, :kept], part, contract, preferred_element_type=jnp.float32)
        for t in range(count):
            total = total + jnp.where(
                tid == half * count + t, wide[t * rows : (t + 1) * rows, :], 0.0
            )
    out_ref[...] = total


def shrink(tenants, shares, meta, own, other, normed):
    return kernel_call(
        functools.partial(shrink_kernel, tenants, shares),
        "shrink_share",
        8,
        [SCALARS, HERE, HERE, HERE],
        jax.ShapeDtypeStruct((2 * ADAPTER_RANK, normed.shape[0]), jnp.float32),
    )(meta, own, other, normed)


def spread_tenants(tenants, parts, rows, meta_ref):
    parts = [part[rows, :] for part in parts]
    while len(parts) > 1:
        parts = [parts[i] + parts[i + 1] for i in range(0, len(parts), 2)]
    shrunk = parts[0]
    rank, tokens = shrunk.shape
    lanes = tenants * rank
    lane = lax.broadcasted_iota(jnp.int32, (rank, lanes), 1)
    repeat = (lane % rank == lax.broadcasted_iota(jnp.int32, (rank, lanes), 0)).astype(
        jnp.bfloat16
    )
    wide = lax.dot_general(
        shrunk.astype(jnp.bfloat16),
        repeat,
        (((0,), (0,)), ((), ())),
        preferred_element_type=jnp.float32,
    )
    index = meta_ref[0] * tokens + lax.broadcasted_iota(jnp.int32, (tokens, 1), 0)
    tid, _ = tenant_at(meta_ref, tenants, index)
    owner = lax.broadcasted_iota(jnp.int32, (1, lanes), 1) // rank
    return jnp.where(owner == tid, wide, 0.0).astype(jnp.bfloat16)


def value_kernel(tenants, shares, meta_ref, *refs):
    parts = refs[:shares]
    own_ref, other_ref, raw_ref, out_ref = refs[shares:]
    side = own_ref.shape[1] - raw_ref.shape[1] // 2
    rank = ADAPTER_RANK
    spread = spread_tenants(tenants, parts, slice(rank, 2 * rank), meta_ref)
    even = lax.rem(meta_ref[0], 2) == 0
    own, other = (
        jnp.concatenate(
            [
                jnp.concatenate(
                    [ref[top : top + rank, side:], ref[top + rank : top + 2 * rank, side:]], axis=1
                )
                for top in range(0, ref.shape[0], 2 * rank)
            ],
            axis=0,
        )
        for ref in (own_ref, other_ref)
    )
    up = jnp.concatenate([jnp.where(even, own, other), jnp.where(even, other, own)], axis=0)
    delta = jnp.dot(spread, up, preferred_element_type=jnp.float32)
    out_ref[...] = (raw_ref[...] + ADAPTER_SCALE * delta).astype(jnp.bfloat16)


def finish_value(tenants, meta, parts, own, other, raw):
    return kernel_call(
        functools.partial(value_kernel, tenants, len(parts)),
        "value_rows",
        5,
        [SCALARS] + [HERE] * (len(parts) + 3),
        jax.ShapeDtypeStruct(raw.shape, jnp.bfloat16),
    )(meta, *parts, own, other, raw)


def query_kernel(tenants, shares, meta_ref, *refs):
    rank = ADAPTER_RANK
    parts = refs[:shares]
    own_ref, other_ref, raw_ref, cos_ref, sin_ref, out_ref = refs[shares:]
    spread = spread_tenants(tenants, parts, slice(0, rank), meta_ref)
    even = lax.rem(meta_ref[0], 2) == 0
    own, other = own_ref[...], other_ref[...]
    up = jnp.concatenate([jnp.where(even, own, other), jnp.where(even, other, own)], axis=0)
    for top in range(0, raw_ref.shape[1], 2 * HEAD_WIDTH):
        delta = jnp.dot(
            spread, up[:, top : top + 2 * HEAD_WIDTH], preferred_element_type=jnp.float32
        )
        for head in range(2):
            local = slice(head * HEAD_WIDTH, (head + 1) * HEAD_WIDTH)
            cols = slice(top + head * HEAD_WIDTH, top + (head + 1) * HEAD_WIDTH)
            row = raw_ref[:, cols] + ADAPTER_SCALE * delta[:, local]
            out_ref[:, cols] = rope(row, cos_ref[...], sin_ref[...]).astype(jnp.bfloat16)


def finish_query(tenants, meta, parts, own, other, raw, cosine, sine):
    return kernel_call(
        functools.partial(query_kernel, tenants, len(parts)),
        "query_rows",
        8,
        [SCALARS] + [HERE] * (len(parts) + 5),
        jax.ShapeDtypeStruct(raw.shape, jnp.bfloat16),
    )(meta, *parts, own, other, raw, cosine, sine)


def tile_bounds(tenants, meta_ref, tokens):
    base = (meta_ref[0] - LONGEST_PROMPT) * tokens
    behind = LONGEST_PROMPT * tokens

    def start_of(index):
        start = 0
        end = 0
        for t in range(tenants):
            end = end + meta_ref[HEADER + t]
            start = jnp.where(index >= end, end, start)
        return start - base

    bounds = []
    for begin in range(behind, behind + tokens, TILE):
        low = start_of(base + begin)
        high = start_of(base + begin + TILE - 1)
        bounds.append((jnp.minimum(low // SLOT, behind // SLOT), high))
    return bounds


def line_up(target, four, two, odd, own):
    tokens = own.shape[0]
    target[:tokens, :] = four[...]
    target[tokens : 2 * tokens, :] = odd[tokens:, :]
    target[2 * tokens : 3 * tokens, :] = two[...]
    target[3 * tokens : 4 * tokens, :] = odd[:tokens, :]
    target[4 * tokens :, :] = own[...]


def head_rows(all_heads, groups):
    width = HEAD_WIDTH
    found = []
    for head in range(all_heads):
        group = head * groups // all_heads
        found.append(
            (
                slice(head * TILE, (head + 1) * TILE),
                slice(head * width, (head + 1) * width),
                slice(group * width, (group + 1) * width),
            )
        )
    return found


def weights_kernel(
    tenants, meta_ref, q_ref, k4, k2, k31, k0, probs, totals, keys, scores, bias, peaks
):
    width = HEAD_WIDTH
    tokens = q_ref.shape[0]
    behind = LONGEST_PROMPT * tokens
    slots = behind // SLOT
    factor = HEAD_WIDTH ** (-0.5) * math.log2(math.e)
    base = (meta_ref[0] - LONGEST_PROMPT) * tokens
    line_up(keys, k4, k2, k31, k0)
    mine = behind + lax.broadcasted_iota(jnp.int32, (tokens, 1), 0)
    _, start = tenant_at(meta_ref, tenants, base + mine)
    start = start - base
    subs = head_rows(q_ref.shape[1] // width, k0.shape[1] // width)
    bounds = tile_bounds(tenants, meta_ref, tokens)

    for tile, (first, high) in enumerate(bounds[:EARLY_TILES]):
        top = slice(tile * TILE, (tile + 1) * TILE)
        odd = lax.rem(first, 2) == 1
        own_slots = (tile + 1) * TILE // SLOT

        def score(slot, count, masked, fresh=False, top=top):
            at_keys = pl.ds(pl.multiple_of(slot * SLOT, SLOT), count * SLOT)
            if masked:
                place = slot * SLOT + lax.broadcasted_iota(jnp.int32, (TILE, count * SLOT), 1)
                seen = (place >= start[top]) & (place <= mine[top])
                bias[:, : count * SLOT] = jnp.where(seen, 0.0, -jnp.inf)
            for at, head, group in subs:
                raw = lax.dot_general(
                    q_ref[top, head],
                    keys[at_keys, group],
                    (((1,), (1,)), ((), ())),
                    preferred_element_type=jnp.float32,
                )
                best = None if fresh else peaks[at, :]
                for piece in range(count * SLOT // width):
                    cols = slice(piece * width, (piece + 1) * width)
                    part = raw[:, cols] * factor
                    if masked:
                        part = part + bias[:, cols]
                    inner = piece * width % SLOT
                    scores[slot + piece * width // SLOT, at, inner : inner + width] = part
                    best = part if best is None else jnp.maximum(best, part)
                peaks[at, :] = best

        def weigh(slot, count, fresh=False, tile=tile):
            for at, _, _ in subs:
                peak = peaks[at, :]
                total = None if fresh else totals[tile, at, :]
                for piece in range(count * SLOT // width):
                    inner = piece * width % SLOT
                    place = slot + piece * width // SLOT
                    weights = jnp.exp2(scores[place, at, inner : inner + width] - peak)
                    total = weights if total is None else total + weights
                    probs[tile, place, at, inner : inner + width] = weights.astype(jnp.bfloat16)
                totals[tile, at, :] = total

        def pair(c, carry, high=high, score=score):
            edge = c * 2 * SLOT < high
            pl.when(edge)(lambda: score(2 * c, 2, True))
            pl.when(jnp.logical_not(edge))(lambda: score(2 * c, 2, False))
            return carry

        def weigh_pair(c, carry, weigh=weigh):
            weigh(2 * c, 2)
            return carry

        score(slots, own_slots, True, fresh=True)
        pl.when(odd)(lambda: score(first, 1, True))
        lax.fori_loop((first + 1) // 2, slots // 2, pair, 0)
        for at, _, _ in subs:
            peaks[at, :] = jnp.broadcast_to(
                jnp.max(peaks[at, :], axis=1, keepdims=True), (TILE, width)
            )
        weigh(slots, own_slots, fresh=True)
        pl.when(odd)(lambda: weigh(first, 1))
        lax.fori_loop((first + 1) // 2, slots // 2, weigh_pair, 0)
        for at, _, _ in subs:
            totals[tile, at, :] = jnp.broadcast_to(
                jnp.sum(totals[tile, at, :], axis=1, keepdims=True), (TILE, width)
            )


def attention_weights(tenants, meta, query, keys):
    tokens, cols = query.shape
    kv_cols = keys[-1].shape[1]
    rows = cols // HEAD_WIDTH * TILE
    span = (LONGEST_PROMPT + 1) * tokens
    slots = span // SLOT
    tiles = EARLY_TILES
    return pl.pallas_call(
        functools.partial(weights_kernel, tenants),
        in_specs=[SCALARS] + [HERE] * (1 + len(keys)),
        out_specs=[HERE, HERE, HERE],
        out_shape=[
            pltpu.VMEM((tiles, slots, rows, SLOT), jnp.bfloat16),
            pltpu.VMEM((tiles, rows, HEAD_WIDTH), jnp.float32),
            pltpu.VMEM((span, kv_cols), jnp.bfloat16),
        ],
        scratch_shapes=[
            pltpu.VMEM((slots, rows, SLOT), jnp.float32),
            pltpu.VMEM((TILE, 2 * SLOT), jnp.float32),
            pltpu.VMEM((rows, HEAD_WIDTH), jnp.float32),
        ],
        compiler_params=pltpu.CompilerParams(vmem_limit_bytes=30 * MIB),
        cost_estimate=pl.CostEstimate(flops=0, bytes_accessed=0, transcendentals=0),
        name="attention_weights",
    )(meta, query, *keys)


def attend_kernel(
    tenants, meta_ref, q_ref, early, early_totals, keys, v4, v2, v31, v0, out_ref,
    values, scores, bias, peaks, totals, mixed,
):
    width = HEAD_WIDTH
    tokens = q_ref.shape[0]
    behind = LONGEST_PROMPT * tokens
    slots = behind // SLOT
    factor = HEAD_WIDTH ** (-0.5) * math.log2(math.e)
    base = (meta_ref[0] - LONGEST_PROMPT) * tokens
    line_up(values, v4, v2, v31, v0)
    mine = behind + lax.broadcasted_iota(jnp.int32, (tokens, 1), 0)
    _, start = tenant_at(meta_ref, tenants, base + mine)
    start = start - base
    subs = head_rows(q_ref.shape[1] // width, v0.shape[1] // width)
    bounds = tile_bounds(tenants, meta_ref, tokens)

    for tile, (first, _) in enumerate(bounds[:EARLY_TILES]):
        top = slice(tile * TILE, (tile + 1) * TILE)

        def mix_early(slot, count, fresh=False, tile=tile):
            at_values = pl.ds(pl.multiple_of(slot * SLOT, SLOT), count * SLOT)
            for at, _, group in subs:
                part = jnp.dot(
                    jnp.concatenate(
                        [early[tile, slot + step, at, :] for step in range(count)], axis=1
                    ),
                    values[at_values, group],
                    preferred_element_type=jnp.float32,
                )
                if fresh:
                    mixed[at, :] = part
                else:
                    mixed[at, :] += part

        def early_pair(c, carry, mix_early=mix_early):
            mix_early(2 * c, 2)
            return carry

        mix_early(slots, (tile + 1) * TILE // SLOT, fresh=True)
        pl.when(lax.rem(first, 2) == 1)(lambda: mix_early(first, 1))
        lax.fori_loop((first + 1) // 2, slots // 2, early_pair, 0)
        for at, head, _ in subs:
            out_ref[top, head] = (mixed[at, :] / early_totals[tile, at, :]).astype(jnp.bfloat16)

    for tile in range(EARLY_TILES, tokens // TILE):
        top = slice(tile * TILE, (tile + 1) * TILE)
        first, high = bounds[tile]
        odd = lax.rem(first, 2) == 1
        own_slots = (tile + 1) * TILE // SLOT

        def columns(slot, count):
            return pl.ds(pl.multiple_of(slot * SLOT, SLOT), count * SLOT)

        def score(slot, count, masked, fresh=False, top=top):
            at_keys = columns(slot, count)
            if masked:
                place = slot * SLOT + lax.broadcasted_iota(jnp.int32, (TILE, count * SLOT), 1)
                seen = (place >= start[top]) & (place <= mine[top])
                bias[:, : count * SLOT] = jnp.where(seen, 0.0, -jnp.inf)
            for at, head, group in subs:
                raw = lax.dot_general(
                    q_ref[top, head],
                    keys[at_keys, group],
                    (((1,), (1,)), ((), ())),
                    preferred_element_type=jnp.float32,
                )
                best = None if fresh else peaks[at, :]
                for piece in range(count * SLOT // width):
                    cols = slice(piece * width, (piece + 1) * width)
                    part = raw[:, cols] * factor
                    if masked:
                        part = part + bias[:, cols]
                    inner = piece * width % SLOT
                    scores[slot + piece * width // SLOT, at, inner : inner + width] = part
                    best = part if best is None else jnp.maximum(best, part)
                peaks[at, :] = best

        def mix(slot, count, fresh=False):
            at_values = columns(slot, count)
            for at, _, group in subs:
                peak = peaks[at, :]
                total = None if fresh else totals[at, :]
                probs = []
                for piece in range(count * SLOT // width):
                    inner = piece * width % SLOT
                    weights = jnp.exp2(
                        scores[slot + piece * width // SLOT, at, inner : inner + width] - peak
                    )
                    total = weights if total is None else total + weights
                    probs.append(weights.astype(jnp.bfloat16))
                totals[at, :] = total
                part = jnp.dot(
                    jnp.concatenate(probs, axis=1),
                    values[at_values, group],
                    preferred_element_type=jnp.float32,
                )
                if fresh:
                    mixed[at, :] = part
                else:
                    mixed[at, :] += part

        def pair(c, carry, high=high, score=score):
            edge = c * 2 * SLOT < high
            pl.when(edge)(lambda: score(2 * c, 2, True))
            pl.when(jnp.logical_not(edge))(lambda: score(2 * c, 2, False))
            return carry

        def mix_pair(c, carry, mix=mix):
            mix(2 * c, 2)
            return carry

        score(slots, own_slots, True, fresh=True)
        pl.when(odd)(lambda: score(first, 1, True))
        lax.fori_loop((first + 1) // 2, slots // 2, pair, 0)
        for at, _, _ in subs:
            peaks[at, :] = jnp.broadcast_to(
                jnp.max(peaks[at, :], axis=1, keepdims=True), (TILE, width)
            )
        mix(slots, own_slots, fresh=True)
        pl.when(odd)(lambda: mix(first, 1))
        lax.fori_loop((first + 1) // 2, slots // 2, mix_pair, 0)
        for at, head, _ in subs:
            total = jnp.sum(totals[at, :], axis=1, keepdims=True)
            out_ref[top, head] = (mixed[at, :] / total).astype(jnp.bfloat16)


def attend(tenants, meta, query, early, early_totals, keys, values):
    tokens, cols = query.shape
    kv_cols = keys.shape[1]
    rows = cols // HEAD_WIDTH * TILE
    span = (LONGEST_PROMPT + 1) * tokens
    return kernel_call(
        functools.partial(attend_kernel, tenants),
        "attention",
        36,
        [SCALARS] + [HERE] * (4 + len(values)),
        jax.ShapeDtypeStruct((tokens, cols), jnp.bfloat16),
        [
            pltpu.VMEM((span, kv_cols), jnp.bfloat16),
            pltpu.VMEM((span // SLOT, rows, SLOT), jnp.float32),
            pltpu.VMEM((TILE, 2 * SLOT), jnp.float32),
            pltpu.VMEM((rows, HEAD_WIDTH), jnp.float32),
            pltpu.VMEM((rows, HEAD_WIDTH), jnp.float32),
            pltpu.VMEM((rows, HEAD_WIDTH), jnp.float32),
        ],
    )(meta, query, early, early_totals, keys, *values)


def after(value, *others):
    return lax.optimization_barrier((value,) + others)[0]


def swap_cores(x):
    peers = lax.axis_size("tok")
    return lax.ppermute(x, "tok", [(i, i ^ 1) for i in range(peers)])


def from_behind(x, by):
    peers = lax.axis_size("tok")
    return lax.ppermute(x, "tok", [(i, i + by) for i in range(peers - by)])


def sent_kernel(meta_ref, own, two, four, out_ref):
    tokens = own.shape[0]
    even = lax.rem(meta_ref[0], 2) == 0
    middle = two[...]
    out_ref[:tokens, :] = jnp.where(even, own[...], middle)
    out_ref[tokens:, :] = jnp.where(even, middle, four[...])


def swap_behind(meta, own, two, four):
    tokens, cols = own.shape
    arrays = [own, two, four]
    sent = kernel_call(
        sent_kernel,
        "sent_blocks",
        5,
        [SCALARS] + [HERE] * len(arrays),
        jax.ShapeDtypeStruct((2 * tokens, cols), own.dtype),
    )(meta, *arrays)
    return swap_cores(sent)


def chip_orders():
    peers = lax.axis_size("tok")
    bits = [1 << b for b in range(1, (peers - 1).bit_length())]
    turn = len(bits) // 2
    orders = (bits, bits[turn:] + bits[:turn])
    return [
        [(i, i ^ orders[i % 2][step]) for i in range(peers)] for step in range(len(bits))
    ]


def body(
    layer_input,
    input_norm_gain,
    query_weight,
    key_weight,
    value_weight,
    query_down_maps,
    value_down_maps,
    query_up_maps,
    value_up_maps,
    tenant_prompt_length,
    tenant_adapter_id,
    adapter_storage_slot,
):
    tok_rows = layer_input.shape[0]
    shares = lax.axis_size("mlp")
    lengths = tenant_prompt_length
    tenants = lengths.shape[0]
    places = jnp.stack([lax.axis_index("tok"), lax.axis_index("mlp"), jnp.int32(tenants)])
    meta = jnp.concatenate([places, lengths, tenant_adapter_id, adapter_storage_slot])
    first, first_sent, second, second_sent, positions = pick(
        tenants, tok_rows, meta, query_down_maps, value_down_maps, query_up_maps, value_up_maps
    )
    orders = chip_orders()
    steps = len(orders)
    cosine, sine = rotary_tables(positions[0])

    def shared(part):
        parts = [part]
        for bit in range(1, shares):
            parts.append(lax.ppermute(part, "mlp", [(i, i ^ bit) for i in range(shares)]))
        return parts

    sum_a = first + swap_cores(first_sent)
    got_a = lax.ppermute(sum_a, "tok", orders[0])
    gain, sum_a = lax.optimization_barrier((input_norm_gain[None, :], sum_a))
    normed, key, raw_value = project_kv(layer_input, gain, key_weight, value_weight, cosine, sine)
    sum_b = second + swap_cores(second_sent)
    got_a, key, sum_b = lax.optimization_barrier((got_a, key, sum_b))
    for step in range(1, steps):
        sum_a = sum_a + got_a
        got_a = lax.ppermute(sum_a, "tok", orders[step])
    normed, sum_a = lax.optimization_barrier((normed, sum_a))
    raw_query = project_query(normed, query_weight)
    got_a, raw_query = lax.optimization_barrier((got_a, raw_query))
    sum_a = sum_a + got_a
    other_a = swap_cores(sum_a)
    sum_b, key = lax.optimization_barrier((sum_b, key, sum_a))[:2]
    got_b = lax.ppermute(sum_b, "tok", orders[0])
    key_four, key_two = from_behind(key, 4), from_behind(key, 2)
    parts = shared(shrink(tenants, shares, meta, sum_a, other_a, normed))
    value = finish_value(tenants, meta, parts, sum_a, other_a, raw_value)
    value_four, value_two = from_behind(value, 4), from_behind(value, 2)
    for step in range(1, steps):
        sum_b = sum_b + got_b
        got_b = lax.ppermute(sum_b, "tok", orders[step])
    sum_b = sum_b + got_b
    other_b = swap_cores(sum_b)
    key_four, key_two = after(key_four, value), after(key_two, value)
    keys = [key_four, key_two, swap_behind(meta, key, key_two, key_four), key]
    query = finish_query(tenants, meta, parts, sum_b, other_b, raw_query, cosine, sine)
    early, totals, lined = attention_weights(tenants, meta, query, keys)
    value_four, value_two, totals = lax.optimization_barrier((value_four, value_two, totals))
    values = [value_four, value_two, swap_behind(meta, value, value_two, value_four), value]
    return attend(tenants, meta, query, early, totals, lined, values)


def solution(mesh):
    placed = (
        P("tok", None),
        P(),
        P(None, "mlp"),
        P(None, "mlp"),
        P(None, "mlp"),
        P("tok", None, "mlp"),
        P("tok", None, "mlp"),
        P("tok", None, "mlp"),
        P("tok", None, "mlp"),
        P(),
        P(),
        P(),
    )
    return jax.shard_map(
        body, mesh=mesh, in_specs=placed, out_specs=P("tok", "mlp"), check_vma=False
    )
```
